32 devices in a mesh: section: 2 (over x), dp: 4 (over z), tensor: 4 (over y, core).
Axes of the slice: x: 2, y: 2, z: 4, core: 2. Of those that a mesh axis runs over, the one named last changes fastest.
Arguments:
- block_input: bfloat16 [3840, 2048], P('dp'), may hold values from -6 to 6
- out_grad: bfloat16 [3840, 2048], P('dp'), may hold values from -6 to 6
- seq_lengths: int32 [4, 4], P('dp'), may hold values from 0 to 960, as said below
- attn_gains: bfloat16 [2, 2048], P('section'), may hold values from 0.099609375 to 1.8984375
- attn_weights: bfloat16 [2, 2, 2048, 2048], P('section', None, None, 'tensor')
- ffn_gain: bfloat16 [2048], replicated, may hold values from 0.099609375 to 1.8984375
- gate_weight: bfloat16 [2048, 5504], P(None, ('section', 'tensor')), may hold values from -0.125 to 0.125
- up_weight: bfloat16 [2048, 5504], P(None, ('section', 'tensor')), may hold values from -0.125 to 0.125
- down_weight: bfloat16 [5504, 2048], P(('section', 'tensor')), may hold values from -0.078125 to 0.078125
Outputs:
- block_output: bfloat16 [3840, 2048], P('dp', ('section', 'tensor'))
- input_grad: bfloat16 [3840, 2048], P('dp', ('section', 'tensor'))
- attn_gains_grad: float32 [2, 2048], P('section')
- attn_weights_grad: float32 [2, 2, 2048, 2048], P('section', None, None, 'tensor')
- ffn_gain_grad: float32 [2048], replicated
- gate_weight_grad: float32 [2048, 5504], P(None, ('section', 'tensor'))
- up_weight_grad: float32 [2048, 5504], P(None, ('section', 'tensor'))
- down_weight_grad: float32 [5504, 2048], P(('section', 'tensor'))
- activation_rms: float32 [2], replicated
The draws below stay inside these ranges and needn't reach their ends.
Inputs may be any that keep to these rules, and one draw needn't show every extreme that they name: `seq_lengths`: row g lists the lengths of group g's sequences, packed in order from the group's first token slot: 1 to 4 positive entries first, zeros after, summing to at most 960; slots past the sum are padding. Some row holds one sequence of 960.
All inputs are finite; a program needn't handle non-finite values.
Results may differ from the reference program's by a relative error of at most 0.017.
Values may be sent and summed in bfloat16 or wider, within the bound.
No kernel may reach another device: no remote copies, remote signals or barrier semaphores. Data moves between devices by JAX's collectives and lax.ppermute only.
A program may use at most 256 MiB of HBM per device.

```python
import jax
import jax.numpy as jnp
from jax import lax

D = 2048
HEADS = 16
HEAD_SIZE = 128
FF = 5504
TOK_DEV = 960
SEQ_SLOTS = 4
GROUPS = 4
TOKENS = 3840


def draw_seq_lengths(key, part):
    key = jax.random.fold_in(key, 11)
    key_count, key_short, key_full, key_share = jax.random.split(key, 4)
    seq_counts = jax.random.randint(key_count, (GROUPS,), 1, SEQ_SLOTS + 1)
    short_by = jax.random.randint(key_short, (GROUPS,), 0, TOK_DEV // 2 + 1)
    full_group = jax.random.randint(key_full, (), 0, GROUPS)
    is_full = jnp.arange(GROUPS, dtype=jnp.int32) == full_group
    group_total = jnp.where(is_full, TOK_DEV, TOK_DEV - short_by)
    seq_counts = jnp.where(is_full, 1, seq_counts)
    seq_shares = jax.random.randint(key_share, (GROUPS, SEQ_SLOTS), 2, 6)
    is_active = jnp.arange(SEQ_SLOTS, dtype=jnp.int32)[None, :] < seq_counts[:, None]
    seq_shares = jnp.where(is_active, seq_shares, 0)
    share_sum = jnp.sum(seq_shares, axis=1, keepdims=True)
    seq_lens = group_total[:, None] * seq_shares // share_sum
    leftover = group_total - jnp.sum(seq_lens, axis=1)
    seq_lens = seq_lens.at[:, 0].add(leftover)
    return seq_lens.astype(jnp.int32)


def draw_attn_weights(key, part):
    key = jax.random.fold_in(key, 7)
    width_all = HEADS * HEAD_SIZE
    base_scale = D ** (-0.5)
    out_scale = max(1, width_all * 16 // TOK_DEV) ** (-0.5)
    out_pick = jnp.zeros((2, 2, 1, 1), jnp.float32).at[1, 1].set(1.0)
    scales = base_scale + (out_scale - base_scale) * out_pick
    raw_noise = jax.random.normal(key, (2, 2, D, width_all), jnp.float32)
    return (raw_noise * scales).astype(jnp.bfloat16)


def block_scale(stream_key, shape, cuts, low, largest):
    def one(axis_at, shards_of):
        steps = jax.random.uniform(jax.random.fold_in(jax.random.fold_in(stream_key, 6), axis_at), (shards_of,), jnp.float32, low / len(cuts), largest / len(cuts))
        return jnp.repeat(jnp.exp(steps), shape[axis_at] // shards_of).reshape((-1,) + (1,) * (len(shape) - axis_at - 1))

    level = one(*cuts[0])
    for cut in cuts[1:]:
        level = level * one(*cut)
    return level


def noise(rng, dims, deviation, most, cuts=(), kind=jnp.bfloat16):
    drawn = deviation * jax.random.normal(rng, dims, jnp.float32)
    if cuts:
        drawn = drawn * block_scale(rng, dims, cuts, -0.22, 0.18)
    return jnp.clip(drawn, -most, most).astype(kind)


def setup_inputs(seed: int = 0) -> dict:
    streams_of = jax.random.split(jax.random.key(seed), 10)
    block_input = noise(streams_of[0], (TOKENS, D), 1.0, 6.0, ((0, 4),))
    out_grad = noise(streams_of[1], (TOKENS, D), 1.0, 6.0, ((0, 4),))
    seq_lengths = draw_seq_lengths(jax.random.fold_in(streams_of[9], 71), 0)
    attn_gains = jnp.clip(1.0 + 0.18 * jax.random.normal(streams_of[3], (2, D), jnp.float32), 0.099609375, 1.8984375).astype(jnp.bfloat16)
    attn_weights = draw_attn_weights(jax.random.fold_in(streams_of[9], 71), 0)
    ffn_gain = jnp.clip(1.0 + 0.18 * jax.random.normal(streams_of[5], (D,), jnp.float32), 0.099609375, 1.8984375).astype(jnp.bfloat16)
    gate_weight = noise(streams_of[6], (D, FF), D ** -0.5, 0.125, ((1, 8),))
    up_weight = noise(streams_of[7], (D, FF), D ** -0.5, 0.125, ((1, 8),))
    down_weight = noise(streams_of[8], (FF, D), FF ** -0.5, 0.078125, ((0, 8),))
    return {"block_input": block_input, "out_grad": out_grad, "seq_lengths": seq_lengths, "attn_gains": attn_gains, "attn_weights": attn_weights, "ffn_gain": ffn_gain, "gate_weight": gate_weight, "up_weight": up_weight, "down_weight": down_weight}


epsilon = 1e-06
highest = lax.Precision.HIGHEST
negative = -1e+30

@jax.custom_vjp
def low(v):
    return lax.optimization_barrier(v.astype(jnp.bfloat16)).astype(jnp.float32)

@jax.custom_vjp
def low_back(v):
    return v

def low_keep(v):
    return (low(v), None)

def low_pass(kept, grad):
    return (grad,)

def back_keep(v):
    return (v, None)

def back_low(kept, grad):
    return (low(grad),)
low.defvjp(low_keep, low_pass)
low_back.defvjp(back_keep, back_low)

def segment_ids(length_row):
    seq_ends = jnp.cumsum(length_row).astype(jnp.int32)
    places = jnp.arange(TOK_DEV, dtype=jnp.int32)
    return lax.optimization_barrier(jnp.sum((places[:, None] >= seq_ends[None, :]).astype(jnp.int32), axis=1)).astype(jnp.int32)

def rms_scale(values_in):
    return lax.rsqrt(lax.optimization_barrier(jnp.mean(values_in * values_in, axis=-1, keepdims=True)) + epsilon)

def group_layer(params, group_item):
    gains, attn, gain_ffn, gate_w, up_w, down_w = params
    tok_rows, seg_row = group_item
    inverse = rms_scale(tok_rows)
    normed_kv = low(tok_rows * inverse * gains[0])
    normed_q = low(tok_rows * inverse * gains[1])
    keys = low_back(low(jnp.dot(normed_kv, attn[0, 0], precision=highest)))
    values = low_back(low(jnp.dot(normed_kv, attn[0, 1], precision=highest)))
    queries = low_back(low(jnp.dot(normed_q, attn[1, 0], precision=highest)))
    head_shape = (TOK_DEV, HEADS, HEAD_SIZE)
    scores = jnp.einsum('qhd,khd->hqk', queries.reshape(head_shape), keys.reshape(head_shape), precision=highest)
    scores = low_back(scores * HEAD_SIZE ** (-0.5))
    places = jnp.arange(TOK_DEV, dtype=jnp.int32)
    allowed = (seg_row[:, None] == seg_row[None, :]) & (places[None, :] <= places[:, None])
    scores = jnp.where(allowed[None], scores, negative)
    maximum = lax.optimization_barrier(jnp.max(scores, axis=-1, keepdims=True))
    exponent = jnp.exp(scores - maximum)
    probs_low = low(exponent / lax.optimization_barrier(jnp.sum(exponent, axis=-1, keepdims=True)))
    mixed = jnp.einsum('hqk,khd->qhd', probs_low, values.reshape(head_shape), precision=highest)
    attn_out = low_back(low(mixed.reshape(TOK_DEV, HEADS * HEAD_SIZE)))
    branch = low_back(jnp.dot(attn_out, attn[1, 1].T, precision=highest))
    residual = tok_rows + branch
    hidden_in = low(residual * rms_scale(residual) * gain_ffn)
    gate_act = low_back(jnp.dot(hidden_in, gate_w, precision=highest))
    up_act = low_back(jnp.dot(hidden_in, up_w, precision=highest))
    hidden = low(jax.nn.silu(gate_act) * up_act)
    layer_sum = residual + jnp.dot(hidden, down_w, precision=highest)
    return (layer_sum, branch)

def reference(block_input, out_grad, seq_lengths, attn_gains, attn_weights, ffn_gain, gate_weight, up_weight, down_weight):
    seg_ids = jax.vmap(segment_ids)(seq_lengths)

    def forward(tok_all, gains, attn, gain_ffn, gate_w, up_w, down_w):
        params = (gains, attn, gain_ffn, gate_w, up_w, down_w)
        layer_fn = jax.checkpoint(lambda group_item: group_layer(params, group_item))
        sums, branches = lax.map(layer_fn, (tok_all.reshape(GROUPS, TOK_DEV, D), seg_ids))
        return (sums.reshape(TOKENS, D), branches.reshape(TOKENS, D))
    primals = [block_input, attn_gains, attn_weights, ffn_gain, gate_weight, up_weight, down_weight]
    primals = [item.astype(jnp.float32) for item in primals]
    layer_sum, pullback, branch = jax.vjp(forward, *primals, has_aux=True)
    grads = pullback(out_grad.astype(jnp.float32))
    is_valid = (seg_ids < SEQ_SLOTS).reshape(TOKENS, 1)
    count_all = jnp.sum(seq_lengths).astype(jnp.float32) * D
    out_sq = jnp.sum(jnp.where(is_valid, layer_sum * layer_sum, 0.0))
    branch_sq = jnp.sum(jnp.where(is_valid, branch * branch, 0.0))
    activation_rms = jnp.sqrt(jnp.stack([out_sq, branch_sq]) / count_all)
    return (layer_sum.astype(jnp.bfloat16), grads[0].astype(jnp.bfloat16), grads[1], grads[2], grads[3], grads[4], grads[5], grads[6], activation_rms)
```

```python
import jax
import jax.numpy as jnp
from jax import lax
from jax.sharding import PartitionSpec as P

HEAD_SIZE = 128
epsilon = 1e-06
negative = -1e30
bf16 = jnp.bfloat16
f32 = jnp.float32

SWAP_SECTION = [(0, 1), (1, 0)]
SWAP_LOW = [(i, i ^ 1) for i in range(4)]
SWAP_HIGH = [(i, i ^ 2) for i in range(4)]
SWAP_BOTH = [(i, i ^ 6) for i in range(8)]


def place():
    section, tensor = lax.axis_index("section"), lax.axis_index("tensor")
    return section, tensor // 2, tensor % 2


def pick(blocks, index):
    return lax.dynamic_index_in_dim(blocks, index, 0, keepdims=False)


def swap_low(value):
    return lax.ppermute(value, "tensor", SWAP_LOW)


def swap_high(value):
    return lax.ppermute(value, "tensor", SWAP_HIGH)


def swap_section(value):
    return lax.ppermute(value, "section", SWAP_SECTION)


def swap_both(value):
    return lax.ppermute(value, ("section", "tensor"), SWAP_BOTH)


def scatter_sum(blocks):
    section, high, low = place()
    pairs = blocks.reshape((4, 2) + blocks.shape[1:])
    kept = lax.dynamic_index_in_dim(pairs, low, 1, keepdims=False)
    sent = lax.dynamic_index_in_dim(pairs, 1 - low, 1, keepdims=False)
    half = (kept.astype(f32) + swap_low(sent).astype(f32)).astype(bf16)

    def toward(a, b):
        return pick(half, (section ^ a) * 2 + (high ^ b))

    from_both = swap_both(toward(1, 1))
    from_section = swap_section(toward(1, 0))
    from_high = swap_high(toward(0, 1))
    return (
        toward(0, 0).astype(f32)
        + from_section.astype(f32)
        + from_high.astype(f32)
        + from_both.astype(f32)
    )


def gather_plane(block):
    section, high, low = place()
    found = [
        (swap_both(block), 1, 1),
        (swap_section(block), 1, 0),
        (swap_high(block), 0, 1),
        (block, 0, 0),
    ]
    rows = block.shape[0]
    whole = jnp.zeros((8 * rows, block.shape[1]), block.dtype)
    for value, a, b in found:
        other = swap_low(value)
        chip = ((section ^ a) * 2 + (high ^ b)) * 2
        whole = lax.dynamic_update_slice(whole, value, ((chip + low) * rows, 0))
        whole = lax.dynamic_update_slice(whole, other, ((chip + 1 - low) * rows, 0))
    return whole


def segment_ids(length_row, tok_count):
    slots = length_row.shape[0]
    upto = jnp.arange(slots)[None, :] <= jnp.arange(slots)[:, None]
    seq_ends = jnp.sum(jnp.where(upto, length_row[None, :], 0), axis=1)
    places = jnp.arange(tok_count, dtype=jnp.int32)
    return jnp.sum((places[:, None] >= seq_ends[None, :]).astype(jnp.int32), axis=1)


def norm_back(source, inverse, gain_vec, grad_in):
    scaled = grad_in * gain_vec
    inner_mean = jnp.mean(scaled * source, axis=-1, keepdims=True)
    return inverse * scaled - source * inverse**3 * inner_mean


def dot(left, right, left_dim, right_dim):
    return lax.dot_general(
        left, right, (((left_dim,), (right_dim,)), ((), ())), preferred_element_type=f32
    )


def heads_of(value):
    return value.reshape(value.shape[0], value.shape[1] // HEAD_SIZE, HEAD_SIZE)


def masked_scores(q_heads, k_heads, seg_ids):
    scores = jnp.einsum("qhd,khd->hqk", q_heads, k_heads, preferred_element_type=f32)
    places = jnp.arange(seg_ids.shape[0], dtype=jnp.int32)
    allowed = (seg_ids[:, None] == seg_ids[None, :]) & (places[None, :] <= places[:, None])
    return jnp.where(allowed[None], scores * HEAD_SIZE ** (-0.5), negative)


def attend_forward(queries, keys, values, seg_ids):
    scores = masked_scores(heads_of(queries), heads_of(keys), seg_ids)
    maximum = jnp.max(scores, axis=-1, keepdims=True)
    exponent = jnp.exp(scores - maximum)
    row_total = jnp.sum(exponent, axis=-1, keepdims=True)
    probs_low = (exponent / row_total).astype(bf16)
    mixed = jnp.einsum("hqk,khd->qhd", probs_low, heads_of(values), preferred_element_type=f32)
    return mixed.astype(bf16).reshape(queries.shape), maximum + jnp.log(row_total)


def attend_backward(queries, keys, values, grad_out, seg_ids, log_total):
    q_heads, k_heads, v_heads, g_heads = (heads_of(v) for v in (queries, keys, values, grad_out))
    probs = jnp.exp(masked_scores(q_heads, k_heads, seg_ids) - log_total)
    grad_probs = jnp.einsum("qhd,khd->hqk", g_heads, v_heads, preferred_element_type=f32)
    inner_sum = jnp.sum(probs * grad_probs, axis=-1, keepdims=True)
    grad_scores = (probs * (grad_probs - inner_sum)).astype(bf16)
    scale = HEAD_SIZE ** (-0.5)
    grad_q = jnp.einsum("hqk,khd->qhd", grad_scores, k_heads, preferred_element_type=f32) * scale
    grad_k = jnp.einsum("hqk,qhd->khd", grad_scores, q_heads, preferred_element_type=f32) * scale
    grad_v = jnp.einsum("hqk,qhd->khd", probs.astype(bf16), g_heads, preferred_element_type=f32)
    return tuple(v.astype(bf16).reshape(queries.shape) for v in (grad_q, grad_k, grad_v))


def sum_groups(*grads):
    return [g.astype(f32) for g in lax.psum(tuple(g.astype(bf16) for g in grads), "dp")]


def shards(
    block_input,
    out_grad,
    seq_lengths,
    attn_gains,
    attn_weights,
    ffn_gain,
    gate_weight,
    up_weight,
    down_weight,
):
    tok_count, width = block_input.shape
    section = lax.axis_index("section")
    is_first = section == 0
    plane = lax.axis_size("section") * lax.axis_size("tensor")
    plane_pos = section * lax.axis_size("tensor") + lax.axis_index("tensor")
    rows, columns = tok_count // plane, width // plane
    row_start = plane_pos * rows

    def own_rows(value):
        return lax.dynamic_slice_in_dim(value, row_start, rows, 0)

    seg_ids = segment_ids(seq_lengths[0], tok_count)
    is_valid = (seg_ids < seq_lengths.shape[1]).astype(f32)[:, None]
    inputs_f = block_input.astype(f32)
    inverse = lax.rsqrt(jnp.mean(inputs_f * inputs_f, axis=-1, keepdims=True) + epsilon)
    gain_row = attn_gains[0].astype(f32)
    normed = (inputs_f * inverse * gain_row).astype(bf16)
    w_first, w_second = attn_weights[0, 0], attn_weights[0, 1]
    half = w_first.shape[1] // 2

    first_proj = dot(normed, w_first, 1, 0).astype(bf16)
    second_proj = dot(normed, w_second, 1, 0).astype(bf16)

    def half_of(value, which):
        return lax.dynamic_slice_in_dim(value, which * half, half, 1)

    first_own, first_met = half_of(first_proj, section), swap_section(half_of(first_proj, 1 - section))
    second_met = lax.ppermute(second_proj[:, half:], "section", [(0, 1)])
    out_weight_met = lax.ppermute(w_second[:, :half], "section", [(1, 0)])
    queries = jnp.where(is_first, first_met, first_own)
    keys = jnp.where(is_first, first_own, first_met)
    values = jnp.where(is_first, second_proj[:, :half], second_met)
    out_weight = jnp.where(is_first, out_weight_met, w_second[:, half:])

    attn_out, log_total = attend_forward(queries, keys, values, seg_ids)
    branch_part = dot(attn_out, out_weight, 1, 1).astype(bf16)
    branch = scatter_sum(branch_part.reshape(plane, rows, width))
    residual = own_rows(block_input).astype(f32) + branch
    resid_inv = lax.rsqrt(jnp.mean(residual * residual, axis=-1, keepdims=True) + epsilon)
    gain_ffn = ffn_gain.astype(f32)
    hidden_in = gather_plane((residual * resid_inv * gain_ffn).astype(bf16))
    branch_sq = jnp.sum(branch * branch * own_rows(is_valid))

    gate_act = dot(hidden_in, gate_weight, 1, 0)
    up_act = dot(hidden_in, up_weight, 1, 0)
    gate_sig = jax.nn.sigmoid(gate_act)
    silu_val = gate_act * gate_sig
    hidden = (silu_val * up_act).astype(bf16)
    grad_hidden = dot(out_grad, down_weight, 1, 1)
    grad_up = (grad_hidden * silu_val).astype(bf16)
    grad_gate = (grad_hidden * up_act * gate_sig * (1.0 + gate_act * (1.0 - gate_sig))).astype(bf16)
    grad_hidden_part = (dot(grad_gate, gate_weight, 1, 1) + dot(grad_up, up_weight, 1, 1)).astype(bf16)
    grad_hidden_in = scatter_sum(grad_hidden_part.reshape(plane, rows, width))
    ffn_gain_term = jnp.sum(grad_hidden_in * residual * resid_inv, axis=0)
    grad_residual = own_rows(out_grad).astype(f32) + norm_back(residual, resid_inv, gain_ffn, grad_hidden_in)
    grad_branch_low = gather_plane(grad_residual.astype(bf16))

    def add_own(part, own):
        mixed = (own_rows(part).astype(f32) + own).astype(bf16)
        return lax.dynamic_update_slice_in_dim(part, mixed, row_start, 0)

    def by_columns(part):
        return part.reshape(tok_count, plane, columns).transpose(1, 0, 2)

    ffn_part = add_own(dot(hidden, down_weight, 1, 0).astype(bf16), residual)
    output_sum = scatter_sum(by_columns(ffn_part))
    block_output = output_sum.astype(bf16)
    output_sq = jnp.sum(output_sum * output_sum * is_valid)

    down_grad, gate_grad, up_grad = sum_groups(
        dot(hidden, out_grad, 0, 0), dot(hidden_in, grad_gate, 0, 0), dot(hidden_in, grad_up, 0, 0)
    )

    grad_attn_out = dot(grad_branch_low, out_weight, 1, 0).astype(bf16)
    grad_q, grad_k, grad_v = attend_backward(queries, keys, values, grad_attn_out, seg_ids, log_total)
    first_back = swap_section(jnp.where(is_first, grad_q, grad_k))
    second_back = swap_section(jnp.where(is_first, attn_out, grad_v))

    def joined(own, met):
        return jnp.concatenate([jnp.where(is_first, own, met), jnp.where(is_first, met, own)], axis=1)

    first_grad = joined(jnp.where(is_first, grad_k, grad_q), first_back)
    second_right = joined(jnp.where(is_first, grad_v, attn_out), second_back)
    second_left = jnp.where(is_first, normed, grad_branch_low)
    value_grad = jnp.where(is_first, second_right, jnp.zeros_like(second_right))
    grad_normed = dot(first_grad, w_first, 1, 1) + dot(value_grad, w_second, 1, 1)
    attn_gain_term = jnp.sum(grad_normed * inputs_f * inverse, axis=0)
    input_part = add_own(norm_back(inputs_f, inverse, gain_row, grad_normed).astype(bf16), grad_residual)
    input_grad = scatter_sum(by_columns(input_part)).astype(bf16)

    first_sum, second_sum, down_grad = lax.optimization_barrier(
        (dot(normed, first_grad, 0, 0), dot(second_left, second_right, 0, 0), down_grad)
    )
    attn_weight_grad = jnp.stack(sum_groups(first_sum, second_sum))[None]

    count_term = jnp.where(plane_pos == 0, jnp.sum(seq_lengths).astype(f32), 0.0)
    section_rows = jnp.where(
        jnp.arange(2, dtype=jnp.int32)[:, None] == section, attn_gain_term[None, :], 0.0
    )
    gain_terms = jnp.concatenate([section_rows, ffn_gain_term[None, :]], axis=0)
    stat_terms = jnp.stack([output_sq, branch_sq, count_term])
    gains, stats = lax.psum((gain_terms, stat_terms), ("section", "dp", "tensor"))
    attn_gain_grad = lax.dynamic_slice_in_dim(gains, section, 1, 0)
    activation_rms = jnp.sqrt(stats[:2] / (stats[2] * width))
    return (
        block_output,
        input_grad,
        attn_gain_grad,
        attn_weight_grad,
        gains[2],
        gate_grad,
        up_grad,
        down_grad,
        activation_rms,
    )


def solution(mesh):
    both = ("section", "tensor")
    in_specs = (
        P("dp", None),
        P("dp", None),
        P("dp", None),
        P("section", None),
        P("section", None, None, "tensor"),
        P(),
        P(None, both),
        P(None, both),
        P(both, None),
    )
    out_specs = (
        P("dp", both),
        P("dp", both),
        P("section", None),
        P("section", None, None, "tensor"),
        P(),
        P(None, both),
        P(None, both),
        P(both, None),
        P(),
    )
    return jax.shard_map(
        shards, mesh=mesh, in_specs=in_specs, out_specs=out_specs, check_vma=False
    )
```

```python
import jax
import jax.numpy as jnp
from jax import lax
from jax.experimental import pallas as pl
from jax.experimental.pallas import tpu as pltpu
from jax.sharding import PartitionSpec as P

HEAD_SIZE = 128
epsilon = 1e-06
negative = -1e30
bf16 = jnp.bfloat16
f32 = jnp.float32

SWAP_SECTION = [(0, 1), (1, 0)]
SWAP_LOW = [(i, i ^ 1) for i in range(4)]
SWAP_HIGH = [(i, i ^ 2) for i in range(4)]
SWAP_BOTH = [(i, i ^ 6) for i in range(8)]


def place():
    section, tensor = lax.axis_index("section"), lax.axis_index("tensor")
    return section, tensor // 2, tensor % 2


def pick(blocks, index):
    return lax.dynamic_index_in_dim(blocks, index, 0, keepdims=False)


def swap_low(value):
    return lax.ppermute(value, "tensor", SWAP_LOW)


def swap_high(value):
    return lax.ppermute(value, "tensor", SWAP_HIGH)


def swap_section(value):
    return lax.ppermute(value, "section", SWAP_SECTION)


def swap_both(value):
    return lax.ppermute(value, ("section", "tensor"), SWAP_BOTH)


def meet(*values):
    return lax.optimization_barrier(values)


def add_low(left, right):
    return (left.astype(f32) + right.astype(f32)).astype(bf16)


def scatter_half(blocks):
    pairs = blocks.reshape((4, 2) + blocks.shape[1:])
    low = place()[2]
    kept = lax.dynamic_index_in_dim(pairs, low, 1, keepdims=False)
    sent = lax.dynamic_index_in_dim(pairs, 1 - low, 1, keepdims=False)
    [half] = meet(add_low(kept, swap_low(sent)))
    return half


def scatter_across(half):
    section, high, _ = place()

    def toward(a, b):
        return pick(half, (section ^ a) * 2 + (high ^ b))

    mid = half.shape[2] // 2
    across = toward(1, 1)
    left_met, right_met = swap_section(across[:, :mid]), swap_high(across[:, mid:])
    return left_met, right_met, toward(1, 0), toward(0, 1), toward(0, 0)


def scatter_last(left_met, right_met, to_section, to_high, own):
    mid = left_met.shape[1]
    to_section = jnp.concatenate([to_section[:, :mid], add_low(to_section[:, mid:], right_met)], axis=1)
    to_high = jnp.concatenate([add_low(to_high[:, :mid], left_met), to_high[:, mid:]], axis=1)
    from_section, from_high = swap_section(to_section), swap_high(to_high)
    return own.astype(f32) + from_section.astype(f32) + from_high.astype(f32)


def scatter_sum(blocks):
    return scatter_last(*scatter_across(scatter_half(blocks)))


def gather_plane(block):
    section, high, low = place()
    rows, width = block.shape
    mid = width // 2
    by_section, by_high = swap_section(block), swap_high(block)
    across_left, across_right = swap_high(by_section[:, :mid]), swap_section(by_high[:, mid:])
    found = [
        (block, 0, 0, 0),
        (by_section, 1, 0, 0),
        (by_high, 0, 1, 0),
        (across_left, 1, 1, 0),
        (across_right, 1, 1, mid),
    ]
    whole = jnp.zeros((8 * rows, width), block.dtype)
    for value, a, b, column in found:
        other = swap_low(value)
        chip = ((section ^ a) * 2 + (high ^ b)) * 2
        whole = lax.dynamic_update_slice(whole, value, ((chip + low) * rows, column))
        whole = lax.dynamic_update_slice(whole, other, ((chip + 1 - low) * rows, column))
    return whole


def tensor_rows(whole):
    rows = whole.shape[0] // lax.axis_size("tensor")
    return lax.dynamic_slice_in_dim(whole, lax.axis_index("tensor") * rows, rows, 0)


def other_groups(slices):
    group, count = lax.axis_index("dp"), slices.shape[0]
    return [pick(slices, group ^ k)[None] for k in range(1, count)]


def by_slice(whole):
    return whole.reshape(lax.axis_size("tensor"), -1, whole.shape[1])


def segment_ids(length_row, tok_count):
    slots = length_row.shape[0]
    upto = jnp.arange(slots)[None, :] <= jnp.arange(slots)[:, None]
    seq_ends = jnp.sum(jnp.where(upto, length_row[None, :], 0), axis=1)
    places = jnp.arange(tok_count, dtype=jnp.int32)
    return jnp.sum((places[:, None] >= seq_ends[None, :]).astype(jnp.int32), axis=1)


def norm_back(source, inverse, gain_vec, grad_in):
    scaled = grad_in * gain_vec
    inner_mean = jnp.mean(scaled * source, axis=-1, keepdims=True)
    return inverse * scaled - source * inverse**3 * inner_mean


def dot(left, right, left_dim, right_dim):
    return lax.dot_general(
        left, right, (((left_dim,), (right_dim,)), ((), ())), preferred_element_type=f32
    )


def feed_forward_grads(order, hidden_blocks, grad_pieces, gate_weight, up_weight, down_weight):
    columns_at_once = 256
    count = len(grad_pieces)
    flat = [(at, i) for at, piece in enumerate(grad_pieces) for i in range(piece.shape[0])]
    starts = [flat.index((at, 0)) for at in range(count)]
    rows, width = hidden_blocks.shape[1:]
    units, steps, block = gate_weight.shape[0], len(flat) // 2, 2 * rows
    chunks = width // columns_at_once

    def kernel(order_ref, hidden_ref, *refs):
        grads, refs = refs[:count], refs[count:]
        weights, outs, kept, refs = refs[:3], refs[3:6], refs[6:9], refs[9:]
        hidden_buf, grad_buf, hidden_cols, grad_cols, row_sems, col_sems = refs
        step = pl.program_id(0)

        def row_copies(at, do):
            slot = lax.rem(at, 2)
            for static_at in range(steps):

                @pl.when(at == static_at)
                def _():
                    for i in range(2):
                        segment = static_at * 2 + i
                        piece, index = flat[segment]
                        found = hidden_ref.at[order_ref[segment]]
                        do(pltpu.make_async_copy(found, hidden_buf.at[slot, i], row_sems.at[slot, 0, i]))
                        found = grads[piece].at[index]
                        do(pltpu.make_async_copy(found, grad_buf.at[slot, i], row_sems.at[slot, 1, i]))

        def col_copies(at, do):
            slot = lax.rem(at, 2)
            columns = pl.ds(pl.multiple_of(at * columns_at_once, columns_at_once), columns_at_once)
            for segment in range(2 * steps):
                found = hidden_ref.at[order_ref[segment], :, columns]
                do(pltpu.make_async_copy(found, hidden_cols.at[slot, segment], col_sems.at[slot, 0, segment]))
            for piece in range(count):
                found = grads[piece].at[:, :, columns]
                into = grad_cols.at[slot, pl.ds(starts[piece], grad_pieces[piece].shape[0])]
                do(pltpu.make_async_copy(found, into, col_sems.at[slot, 1, piece]))

        @pl.when(step == 0)
        def _():
            row_copies(step, lambda c: c.start())

        @pl.when(step + 1 < steps)
        def _():
            row_copies(step + 1, lambda c: c.start())

        @pl.when(step == steps - 1)
        def _():
            col_copies(0, lambda c: c.start())

        @pl.when(step < steps)
        def _():
            row_copies(step, lambda c: c.wait())
            slot = lax.rem(step, 2)
            h = hidden_buf[slot].reshape(block, width)
            o = grad_buf[slot].reshape(block, width)
            gate = dot(weights[0][...], h, 1, 1)
            up = dot(weights[1][...], h, 1, 1)
            back = dot(weights[2][...], o, 1, 1)
            sig = jax.nn.sigmoid(gate)
            silu = gate * sig
            kept[0][step] = (silu * up).astype(bf16)
            kept[1][step] = (back * up * sig * (1.0 + gate * (1.0 - sig))).astype(bf16)
            kept[2][step] = (back * silu).astype(bf16)

        @pl.when(step >= steps)
        def _():
            chunk = step - steps
            col_copies(chunk, lambda c: c.wait())

            @pl.when(chunk + 1 < chunks)
            def _():
                col_copies(chunk + 1, lambda c: c.start())

            slot = lax.rem(chunk, 2)
            h = hidden_cols[slot].reshape(steps * block, columns_at_once)
            o = grad_cols[slot].reshape(steps * block, columns_at_once)
            for i, right in ((0, o), (1, h), (2, h)):
                parts = [dot(kept[i][j], right[j * block : (j + 1) * block], 1, 0) for j in range(steps)]
                outs[i][...] = sum(parts[1:], parts[0])

    anywhere = pl.BlockSpec(memory_space=pl.ANY)
    weight = pl.BlockSpec((units, width), lambda i, order: (0, 0), pipeline_mode=pl.Buffered(1))
    result = pl.BlockSpec((units, columns_at_once), lambda i, order: (0, jnp.maximum(i - steps, 0)))
    whole_rows = pltpu.VMEM((2, 2, rows, width), bf16)
    some_columns = pltpu.VMEM((2, 2 * steps, rows, columns_at_once), bf16)
    return pl.pallas_call(
        kernel,
        out_shape=[jax.ShapeDtypeStruct((units, width), f32)] * 3,
        grid_spec=pltpu.PrefetchScalarGridSpec(
            num_scalar_prefetch=1,
            grid=(steps + chunks,),
            in_specs=[anywhere] * (1 + count) + [weight] * 3,
            out_specs=[result] * 3,
            scratch_shapes=[pltpu.VMEM((steps, units, block), bf16)] * 3
            + [whole_rows, whole_rows, some_columns, some_columns]
            + [pltpu.SemaphoreType.DMA((2, 2, 2)), pltpu.SemaphoreType.DMA((2, 2, 2 * steps))],
        ),
        compiler_params=pltpu.CompilerParams(vmem_limit_bytes=60 * 2**20),
        name="feed_forward_grads",
    )(order, hidden_blocks, *grad_pieces, gate_weight, up_weight, down_weight)


def whole_block(shape):
    return pl.BlockSpec(shape, lambda *_: (0,) * len(shape), pipeline_mode=pl.Buffered(1))


def kernel_params(mebibytes=56):
    return pltpu.CompilerParams(vmem_limit_bytes=mebibytes * 2**20)


def row_scale(value):
    return lax.rsqrt(jnp.mean(value * value, axis=-1, keepdims=True) + epsilon)


def normed_projections(inputs, gain_row, weights):
    tok_count, width = inputs.shape
    rows, half = tok_count // 4, weights.shape[2] // 2

    def kernel(inputs_ref, gain_ref, weights_ref, normed_ref, first_ref, second_ref):
        value = inputs_ref[...].astype(f32)
        normed = (value * row_scale(value) * gain_ref[...]).astype(bf16)
        normed_ref[...] = normed
        for which, out in enumerate((first_ref, second_ref)):
            product = dot(normed, weights_ref[which], 1, 0).astype(bf16)
            out[0] = product[:, :half]
            out[1] = product[:, half:]

    halves = jax.ShapeDtypeStruct((2, tok_count, half), bf16)
    halves_block = pl.BlockSpec((2, rows, half), lambda i: (0, i, 0))
    row_block = pl.BlockSpec((rows, width), lambda i: (i, 0))
    return pl.pallas_call(
        kernel,
        out_shape=[jax.ShapeDtypeStruct(inputs.shape, bf16), halves, halves],
        grid=(4,),
        in_specs=[row_block, whole_block((1, width)), whole_block(weights.shape)],
        out_specs=[row_block, halves_block, halves_block],
        compiler_params=kernel_params(),
        name="normed_projections",
    )(inputs, gain_row[None], weights)


def allowed_pairs(seg_column, seg_row, start, rows):
    last = start + rows
    shape = (rows, last)
    places = lax.broadcasted_iota(jnp.int32, shape, 0) + start
    causal = lax.broadcasted_iota(jnp.int32, shape, 1) <= places
    return causal & (seg_column[start:last] == seg_row[:, :last])


def attend_forward(queries, keys, values, out_weight, seg_ids):
    tok_count, flat = queries.shape
    width, heads, rows = out_weight.shape[0], flat // HEAD_SIZE, tok_count // 4

    def kernel(q_ref, k_ref, v_ref, weight_ref, column_ref, row_ref, out_ref, branch_ref, log_ref):
        seg_column, seg_row = column_ref[...], row_ref[...]
        for start in range(0, tok_count, rows):
            last = start + rows
            allowed = allowed_pairs(seg_column, seg_row, start, rows)
            for head in range(heads):
                at = slice(head * HEAD_SIZE, (head + 1) * HEAD_SIZE)
                scores = dot(q_ref[start:last, at], k_ref[:last, at], 1, 1) * HEAD_SIZE ** (-0.5)
                scores = jnp.where(allowed, scores, negative)
                maximum = jnp.max(scores, axis=-1, keepdims=True)
                exponent = jnp.exp(scores - maximum)
                total = jnp.sum(exponent, axis=-1, keepdims=True)
                probs = (exponent * (1.0 / total)).astype(bf16)
                out_ref[start:last, at] = dot(probs, v_ref[:last, at], 1, 0).astype(bf16)
                log_ref[head, start:last] = maximum + jnp.log(total)
            branch_ref[start:last] = dot(out_ref[start:last], weight_ref[...], 1, 1).astype(bf16)

    shapes = [(tok_count, flat), (tok_count, width), (heads, tok_count, 1)]
    return pl.pallas_call(
        kernel,
        out_shape=[jax.ShapeDtypeStruct(s, k) for s, k in zip(shapes, (bf16, bf16, f32))],
        compiler_params=kernel_params(),
        name="attend_forward",
    )(queries, keys, values, out_weight, seg_ids[:, None], seg_ids[None])


def attend_backward(queries, keys, values, out_weight, grad_branch, seg_ids, log_total):
    tok_count, flat = queries.shape
    heads, rows = flat // HEAD_SIZE, tok_count // 4
    scale = HEAD_SIZE ** (-0.5)

    def kernel(q_ref, k_ref, v_ref, weight_ref, branch_ref, column_ref, row_ref, log_ref, dq_ref, dk_ref, dv_ref, dk_sum, dv_sum):
        seg_column, seg_row = column_ref[...], row_ref[...]
        dk_sum[...] = jnp.zeros_like(dk_sum)
        dv_sum[...] = jnp.zeros_like(dv_sum)
        for start in range(0, tok_count, rows):
            last = start + rows
            allowed = allowed_pairs(seg_column, seg_row, start, rows)
            grad_out = dot(branch_ref[start:last], weight_ref[...], 1, 0).astype(bf16)
            for head in range(heads):
                at = slice(head * HEAD_SIZE, (head + 1) * HEAD_SIZE)
                scores = dot(q_ref[start:last, at], k_ref[:last, at], 1, 1) * scale
                probs = jnp.exp(jnp.where(allowed, scores, negative) - log_ref[head, start:last])
                grad_probs = dot(grad_out[:, at], v_ref[:last, at], 1, 1)
                inner = jnp.sum(probs * grad_probs, axis=-1, keepdims=True)
                grad_scores = (probs * (grad_probs - inner)).astype(bf16)
                dq_ref[start:last, at] = (dot(grad_scores, k_ref[:last, at], 1, 0) * scale).astype(bf16)
                dk_sum[:last, at] += dot(grad_scores, q_ref[start:last, at], 0, 0)
                dv_sum[:last, at] += dot(probs.astype(bf16), grad_out[:, at], 0, 0)
        dk_ref[...] = (dk_sum[...] * scale).astype(bf16)
        dv_ref[...] = dv_sum[...].astype(bf16)

    return pl.pallas_call(
        kernel,
        out_shape=[jax.ShapeDtypeStruct((tok_count, flat), bf16)] * 3,
        scratch_shapes=[pltpu.VMEM((tok_count, flat), f32)] * 2,
        compiler_params=kernel_params(),
        name="attend_backward",
    )(queries, keys, values, out_weight, grad_branch, seg_ids[:, None], seg_ids[None], log_total)


def feed_forward_own(hidden_in, grad_hidden, gate_weight, up_weight):
    tok_count, width = hidden_in.shape
    units, rows = gate_weight.shape[0], tok_count // 4

    def kernel(in_ref, back_ref, gate_ref, up_ref, hidden_ref, grad_ref):
        gate = dot(in_ref[...], gate_ref[...], 1, 1)
        up = dot(in_ref[...], up_ref[...], 1, 1)
        back = back_ref[...]
        sig = jax.nn.sigmoid(gate)
        silu = gate * sig
        hidden_ref[...] = (silu * up).astype(bf16)
        grad_up = (back * silu).astype(bf16)
        grad_gate = (back * up * sig * (1.0 + gate * (1.0 - sig))).astype(bf16)
        grad = dot(grad_gate, gate_ref[...], 1, 0) + dot(grad_up, up_ref[...], 1, 0)
        grad_ref[...] = grad.astype(bf16)

    row_block = pl.BlockSpec((rows, width), lambda i: (i, 0))
    unit_block = pl.BlockSpec((rows, units), lambda i: (i, 0))
    weight = whole_block((units, width))
    return pl.pallas_call(
        kernel,
        out_shape=[jax.ShapeDtypeStruct((tok_count, units), bf16), jax.ShapeDtypeStruct((tok_count, width), bf16)],
        grid=(4,),
        in_specs=[row_block, unit_block, weight, weight],
        out_specs=[unit_block, row_block],
        compiler_params=kernel_params(),
        name="feed_forward_own",
    )(hidden_in, grad_hidden, gate_weight, up_weight)


def input_gradient(inputs, gain_row, first_grad, value_grad, weights, parts):
    tok_count, width = inputs.shape
    rows, columns, inner = tok_count // 4, width // parts, first_grad.shape[1]

    def kernel(inputs_ref, gain_ref, first_ref, value_ref, weights_ref, out_ref, gain_out):
        grad = dot(first_ref[...], weights_ref[0], 1, 1) + dot(value_ref[...], weights_ref[1], 1, 1)
        value = inputs_ref[...].astype(f32)
        inverse = row_scale(value)
        normal = value * inverse

        @pl.when(pl.program_id(0) == 0)
        def _():
            gain_out[...] = jnp.zeros_like(gain_out)

        gain_out[...] += jnp.sum(grad * normal, axis=0, keepdims=True)
        scaled = grad * gain_ref[...]
        inner_mean = jnp.mean(scaled * value, axis=-1, keepdims=True)
        result = (inverse * scaled - value * (inverse * inverse * inverse * inner_mean)).astype(bf16)
        for part in range(parts):
            out_ref[part] = result[:, part * columns : (part + 1) * columns]

    row_block = pl.BlockSpec((rows, width), lambda i: (i, 0))
    grad_block = pl.BlockSpec((rows, inner), lambda i: (i, 0))
    return pl.pallas_call(
        kernel,
        out_shape=[jax.ShapeDtypeStruct((parts, tok_count, columns), bf16), jax.ShapeDtypeStruct((1, width), f32)],
        grid=(4,),
        in_specs=[row_block, whole_block((1, width)), grad_block, grad_block, whole_block(weights.shape)],
        out_specs=[pl.BlockSpec((parts, rows, columns), lambda i: (0, i, 0)), pl.BlockSpec((1, width), lambda i: (0, 0))],
        compiler_params=kernel_params(),
        name="input_gradient",
    )(inputs, gain_row[None], first_grad, value_grad, weights)


def output_parts(hidden, down_weight, parts):
    tok_count, units = hidden.shape
    columns = down_weight.shape[1] // parts

    def kernel(hidden_ref, weight_ref, out_ref):
        out_ref[0] = dot(hidden_ref[...], weight_ref[...], 1, 0).astype(bf16)

    return pl.pallas_call(
        kernel,
        out_shape=jax.ShapeDtypeStruct((parts, tok_count, columns), bf16),
        grid=(parts,),
        in_specs=[whole_block((tok_count, units)), pl.BlockSpec((units, columns), lambda i: (0, i))],
        out_specs=pl.BlockSpec((1, tok_count, columns), lambda i: (i, 0, 0)),
        compiler_params=kernel_params(),
        name="output_parts",
    )(hidden, down_weight)


def gathers(group_count):
    return group_count in (2, 4)


def sum_plane(value):
    value = value + swap_section(value)
    both = lax.ppermute(value, "tensor", [(i, i ^ 3) for i in range(4)])
    return value, swap_low(value), swap_high(value), both


def sum_pairs(terms):
    return (terms[0] + terms[1]) + (terms[2] + terms[3])


def sum_over_groups(value):
    count = lax.axis_size("dp")

    def across(distance):
        return lax.ppermute(value, "dp", [(i, i ^ distance) for i in range(count)])

    if count == 4:
        return sum_pairs([value, across(1), across(2), across(3)])
    if count & (count - 1):
        return lax.psum(value, "dp")
    for bit in range(count.bit_length() - 1):
        value = value + across(2**bit)
    return value


def sum_groups(*grads):
    return [g.astype(f32) for g in lax.psum(tuple(g.astype(bf16) for g in grads), "dp")]


def shards(
    block_input,
    out_grad,
    seq_lengths,
    attn_gains,
    attn_weights,
    ffn_gain,
    gate_weight,
    up_weight,
    down_weight,
):
    tok_count, width = block_input.shape
    section = lax.axis_index("section")
    is_first = section == 0
    plane = lax.axis_size("section") * lax.axis_size("tensor")
    plane_pos = section * lax.axis_size("tensor") + lax.axis_index("tensor")
    rows, columns = tok_count // plane, width // plane
    row_start = plane_pos * rows

    def own_rows(value):
        return lax.dynamic_slice_in_dim(value, row_start, rows, 0)

    all_tokens = gathers(lax.axis_size("dp"))
    grad_slices, grad_near = None, []
    if all_tokens:
        grad_slice, block_input = meet(tensor_rows(out_grad), block_input)
        grad_slices = lax.all_gather(grad_slice, "dp", axis=0, tiled=False)
    seg_ids = segment_ids(seq_lengths[0], tok_count)
    is_valid = (seg_ids < seq_lengths.shape[1]).astype(f32)[:, None]
    gain_row = attn_gains[0].astype(f32)
    weights = attn_weights[0]
    w_second = weights[1]
    half = weights.shape[2] // 2
    normed, first_proj, second_proj = normed_projections(block_input, gain_row, weights)

    first_own, first_met = pick(first_proj, section), swap_section(pick(first_proj, 1 - section))
    second_met = lax.ppermute(second_proj[1], "section", [(0, 1)])
    out_weight_met = lax.ppermute(w_second[:, :half], "section", [(1, 0)])
    queries = jnp.where(is_first, first_met, first_own)
    keys = jnp.where(is_first, first_own, first_met)
    values = jnp.where(is_first, second_proj[0], second_met)
    out_weight = jnp.where(is_first, out_weight_met, w_second[:, half:])

    attn_out, branch_part, log_total = attend_forward(queries, keys, values, out_weight, seg_ids)
    branch = scatter_sum(branch_part.reshape(plane, rows, width))
    branch, grad_slices = meet(branch, grad_slices)
    residual = own_rows(block_input).astype(f32) + branch
    resid_inv = lax.rsqrt(jnp.mean(residual * residual, axis=-1, keepdims=True) + epsilon)
    gain_ffn = ffn_gain.astype(f32)
    hidden_block = (residual * resid_inv * gain_ffn).astype(bf16)
    hidden_in = gather_plane(hidden_block)
    if all_tokens:
        hidden_block, grad_slices = meet(hidden_block, grad_slices)
        hidden_all = lax.all_gather(hidden_block, ("dp", "section", "tensor"), axis=0, tiled=True)
        grad_near = other_groups(grad_slices)
        grad_near, hidden_in = meet(grad_near, hidden_in)
    branch_sq = jnp.sum(branch * branch * own_rows(is_valid))

    def whole_units(hidden_in, out_grad):
        gate_act, up_act = dot(hidden_in, gate_weight, 1, 0), dot(hidden_in, up_weight, 1, 0)
        grad_hidden = dot(out_grad, down_weight, 1, 1)
        sig = jax.nn.sigmoid(gate_act)
        hidden = (gate_act * sig * up_act).astype(bf16)
        grad_up = (grad_hidden * gate_act * sig).astype(bf16)
        grad_gate = (grad_hidden * up_act * sig * (1.0 + gate_act * (1.0 - sig))).astype(bf16)
        return dot(hidden, out_grad, 0, 0), dot(hidden_in, grad_gate, 0, 0), dot(hidden_in, grad_up, 0, 0)

    gate_units, up_units = gate_weight.T, up_weight.T
    hidden, grad_hidden_part = feed_forward_own(hidden_in, dot(out_grad, down_weight, 1, 1), gate_units, up_units)
    grad_half, hidden = meet(scatter_half(grad_hidden_part.reshape(plane, rows, width)), hidden)
    grad_terms, output_part = meet(scatter_across(grad_half), output_parts(hidden, down_weight, plane))
    grad_hidden_in = scatter_last(*grad_terms)
    ffn_gain_term = jnp.sum(grad_hidden_in * residual * resid_inv, axis=0)
    grad_residual = own_rows(out_grad).astype(f32) + norm_back(residual, resid_inv, gain_ffn, grad_hidden_in)
    grad_branch_low = gather_plane(grad_residual.astype(bf16))
    if all_tokens:
        grad_near, grad_branch_low = meet(grad_near, grad_branch_low)
        grad_high = [swap_high(grad_near[0])]

    def add_own(parts, own):
        own = own.reshape(rows, plane, columns).transpose(1, 0, 2)
        mixed = (lax.dynamic_slice_in_dim(parts, row_start, rows, 1).astype(f32) + own).astype(bf16)
        return lax.dynamic_update_slice_in_dim(parts, mixed, row_start, 1)

    output_half = scatter_half(add_own(output_part, residual))
    grad_q, grad_k, grad_v = attend_backward(
        queries, keys, values, out_weight, grad_branch_low, seg_ids, log_total
    )
    second_back = swap_section(jnp.where(is_first, attn_out, grad_v))

    def joined(own, met):
        return jnp.concatenate([jnp.where(is_first, own, met), jnp.where(is_first, met, own)], axis=1)

    second_right = joined(jnp.where(is_first, grad_v, attn_out), second_back)
    second_left = jnp.where(is_first, normed, grad_branch_low)
    second_sum = dot(second_left, second_right, 0, 0).astype(bf16)
    if len(grad_near) > 1:
        second_back, grad_high, grad_near[1] = meet(second_back, grad_high, grad_near[1])
        grad_high.append(swap_high(grad_near[1]))
    first_back = swap_section(jnp.where(is_first, grad_q, grad_k))
    if len(grad_near) > 2:
        first_back, grad_high, grad_near[2] = meet(first_back, grad_high, grad_near[2])
        grad_high.append(swap_high(grad_near[2]))
    first_grad = joined(jnp.where(is_first, grad_k, grad_q), first_back)
    value_grad = jnp.where(is_first, second_right, jnp.zeros_like(second_right))
    first_sum = dot(normed, first_grad, 0, 0).astype(bf16)
    output_half, first_sum, second_sum = meet(output_half, first_sum, second_sum)
    output_terms = scatter_across(output_half)
    if all_tokens:
        first_sum, second_sum, hidden_all = meet(first_sum, second_sum, hidden_all)
        grad_pieces = [by_slice(out_grad)] + grad_near + grad_high
        grad_pieces += [swap_low(v) for v in grad_near] + [swap_low(v) for v in grad_high]
        tensor, group, groups = lax.axis_index("tensor"), lax.axis_index("dp"), lax.axis_size("dp")
        order = [group * 4 + i for i in range(4)]
        order += [(group ^ k) * 4 + (tensor ^ i) for i in (0, 2, 1, 3) for k in range(1, groups)]
        down_grad, gate_grad, up_grad = feed_forward_grads(
            jnp.stack(order).astype(jnp.int32),
            hidden_all.reshape(4 * groups, -1, width),
            grad_pieces,
            gate_units,
            up_units,
            down_weight,
        )
        output_terms, first_grad, value_grad, down_grad = meet(output_terms, first_grad, value_grad, down_grad)
        gate_grad, up_grad = gate_grad.T, up_grad.T
    else:
        down_grad, gate_grad, up_grad = sum_groups(*whole_units(hidden_in, out_grad))
    input_part, attn_gain_term = input_gradient(block_input, gain_row, first_grad, value_grad, weights, plane)
    input_terms = scatter_across(scatter_half(add_own(input_part, grad_residual)))
    output_sum = scatter_last(*output_terms)
    block_output = output_sum.astype(bf16)
    output_sq = jnp.sum(output_sum * output_sum * is_valid)

    count_term = jnp.where(plane_pos == 0, jnp.sum(seq_lengths).astype(f32), 0.0)
    section_rows = jnp.where(
        jnp.arange(2, dtype=jnp.int32)[:, None] == section, attn_gain_term, 0.0
    )
    stat_terms = jnp.pad(jnp.stack([output_sq, branch_sq, count_term]), (0, width - 3))
    terms = jnp.concatenate([section_rows, ffn_gain_term[None, :], stat_terms[None, :]], axis=0)
    gains = sum_plane(terms)
    first_sum, second_sum = lax.psum((first_sum, second_sum), "dp")
    if all_tokens:
        first_sum, second_sum, input_terms, gains = meet(first_sum, second_sum, input_terms, gains)
    input_grad = scatter_last(*input_terms).astype(bf16)
    gains = sum_over_groups(sum_pairs(gains))
    attn_weight_grad = jnp.stack([first_sum, second_sum])[None].astype(f32)

    stats = gains[3]
    attn_gain_grad = lax.dynamic_slice_in_dim(gains, section, 1, 0)
    activation_rms = jnp.sqrt(stats[:2] / (stats[2] * width))
    return (
        block_output,
        input_grad,
        attn_gain_grad,
        attn_weight_grad,
        gains[2],
        gate_grad,
        up_grad,
        down_grad,
        activation_rms,
    )


def solution(mesh):
    both = ("section", "tensor")
    in_specs = (
        P("dp", None),
        P("dp", None),
        P("dp", None),
        P("section", None),
        P("section", None, None, "tensor"),
        P(),
        P(None, both),
        P(None, both),
        P(both, None),
    )
    out_specs = (
        P("dp", both),
        P("dp", both),
        P("section", None),
        P("section", None, None, "tensor"),
        P(),
        P(None, both),
        P(None, both),
        P(both, None),
        P(),
    )
    return jax.shard_map(
        shards, mesh=mesh, in_specs=in_specs, out_specs=out_specs, check_vma=False
    )
```

```python
import jax
import jax.numpy as jnp
from jax import lax
from jax.experimental import pallas as pl
from jax.experimental.pallas import tpu as pltpu
from jax.sharding import PartitionSpec as P

HEAD_SIZE = 128
epsilon = 1e-06
negative = -1e30
bf16 = jnp.bfloat16
f32 = jnp.float32

SWAP_SECTION = [(0, 1), (1, 0)]
SWAP_LOW = [(i, i ^ 1) for i in range(4)]
SWAP_HIGH = [(i, i ^ 2) for i in range(4)]
SWAP_BOTH = [(i, i ^ 6) for i in range(8)]


def place():
    section, tensor = lax.axis_index("section"), lax.axis_index("tensor")
    return section, tensor // 2, tensor % 2


def pick(blocks, index):
    return lax.dynamic_index_in_dim(blocks, index, 0, keepdims=False)


def swap_low(value):
    return lax.ppermute(value, "tensor", SWAP_LOW)


def swap_high(value):
    return lax.ppermute(value, "tensor", SWAP_HIGH)


def swap_section(value):
    return lax.ppermute(value, "section", SWAP_SECTION)


def swap_both(value):
    return lax.ppermute(value, ("section", "tensor"), SWAP_BOTH)


def meet(*values):
    return lax.optimization_barrier(values)


def add_low(left, right):
    return (left.astype(f32) + right.astype(f32)).astype(bf16)


def scatter_half(blocks):
    pairs = blocks.reshape((4, 2) + blocks.shape[1:])
    low = place()[2]
    kept = lax.dynamic_index_in_dim(pairs, low, 1, keepdims=False)
    sent = lax.dynamic_index_in_dim(pairs, 1 - low, 1, keepdims=False)
    [half] = meet(add_low(kept, swap_low(sent)))
    return half


def scatter_across(half):
    section, high, _ = place()

    def toward(a, b):
        return pick(half, (section ^ a) * 2 + (high ^ b))

    mid = half.shape[2] // 2
    across = toward(1, 1)
    left_met, right_met = swap_section(across[:, :mid]), swap_high(across[:, mid:])
    return left_met, right_met, toward(1, 0), toward(0, 1), toward(0, 0)


def scatter_last(left_met, right_met, to_section, to_high, own):
    mid = left_met.shape[1]
    to_section = jnp.concatenate([to_section[:, :mid], add_low(to_section[:, mid:], right_met)], axis=1)
    to_high = jnp.concatenate([add_low(to_high[:, :mid], left_met), to_high[:, mid:]], axis=1)
    from_section, from_high = swap_section(to_section), swap_high(to_high)
    return own.astype(f32) + from_section.astype(f32) + from_high.astype(f32)


def scatter_sum(blocks):
    return scatter_last(*scatter_across(scatter_half(blocks)))


def gather_plane(block):
    section, high, low = place()
    rows, width = block.shape
    mid = width // 2
    by_section, by_high = swap_section(block), swap_high(block)
    across_left, across_right = swap_high(by_section[:, :mid]), swap_section(by_high[:, mid:])
    found = [
        (block, 0, 0, 0),
        (by_section, 1, 0, 0),
        (by_high, 0, 1, 0),
        (across_left, 1, 1, 0),
        (across_right, 1, 1, mid),
    ]
    whole = jnp.zeros((8 * rows, width), block.dtype)
    for value, a, b, column in found:
        other = swap_low(value)
        chip = ((section ^ a) * 2 + (high ^ b)) * 2
        whole = lax.dynamic_update_slice(whole, value, ((chip + low) * rows, column))
        whole = lax.dynamic_update_slice(whole, other, ((chip + 1 - low) * rows, column))
    return whole


def tensor_rows(whole, other=0):
    rows = whole.shape[0] // lax.axis_size("tensor")
    return lax.dynamic_slice_in_dim(whole, (lax.axis_index("tensor") ^ other) * rows, rows, 0)


def other_groups(slices):
    group, count = lax.axis_index("dp"), slices.shape[0]
    return [pick(slices, group ^ k)[None] for k in range(1, count)]


def by_slice(whole):
    return whole.reshape(lax.axis_size("tensor"), -1, whole.shape[1])


def segment_ids(length_row, tok_count):
    slots = length_row.shape[0]
    upto = jnp.arange(slots)[None, :] <= jnp.arange(slots)[:, None]
    seq_ends = jnp.sum(jnp.where(upto, length_row[None, :], 0), axis=1)
    places = jnp.arange(tok_count, dtype=jnp.int32)
    return jnp.sum((places[:, None] >= seq_ends[None, :]).astype(jnp.int32), axis=1)


def norm_back(source, inverse, gain_vec, grad_in):
    scaled = grad_in * gain_vec
    inner_mean = jnp.mean(scaled * source, axis=-1, keepdims=True)
    return inverse * scaled - source * inverse**3 * inner_mean


def dot(left, right, left_dim, right_dim):
    return lax.dot_general(
        left, right, (((left_dim,), (right_dim,)), ((), ())), preferred_element_type=f32
    )


def feed_forward_grads(order, hidden_blocks, grad_pieces, gate_weight, up_weight, down_weight):
    columns_at_once = 256
    count = len(grad_pieces)
    flat = [(at, i) for at, piece in enumerate(grad_pieces) for i in range(piece.shape[0])]
    starts = [flat.index((at, 0)) for at in range(count)]
    rows, width = hidden_blocks.shape[1:]
    units, steps, block = gate_weight.shape[0], len(flat) // 2, 2 * rows
    chunks = width // columns_at_once

    def kernel(order_ref, hidden_ref, *refs):
        grads, refs = refs[:count], refs[count:]
        weights, outs, kept, refs = refs[:3], refs[3:6], refs[6:9], refs[9:]
        hidden_buf, grad_buf, hidden_cols, grad_cols, row_sems, col_sems = refs
        step = pl.program_id(0)

        def row_copies(at, do):
            slot = lax.rem(at, 2)
            for static_at in range(steps):

                @pl.when(at == static_at)
                def _():
                    for i in range(2):
                        segment = static_at * 2 + i
                        piece, index = flat[segment]
                        found = hidden_ref.at[order_ref[segment]]
                        do(pltpu.make_async_copy(found, hidden_buf.at[slot, i], row_sems.at[slot, 0, i]))
                        found = grads[piece].at[index]
                        do(pltpu.make_async_copy(found, grad_buf.at[slot, i], row_sems.at[slot, 1, i]))

        def col_copies(at, do):
            slot = lax.rem(at, 2)
            columns = pl.ds(pl.multiple_of(at * columns_at_once, columns_at_once), columns_at_once)
            for segment in range(2 * steps):
                found = hidden_ref.at[order_ref[segment], :, columns]
                do(pltpu.make_async_copy(found, hidden_cols.at[slot, segment], col_sems.at[slot, 0, segment]))
            for piece in range(count):
                found = grads[piece].at[:, :, columns]
                into = grad_cols.at[slot, pl.ds(starts[piece], grad_pieces[piece].shape[0])]
                do(pltpu.make_async_copy(found, into, col_sems.at[slot, 1, piece]))

        @pl.when(step == 0)
        def _():
            row_copies(step, lambda c: c.start())

        @pl.when(step + 1 < steps)
        def _():
            row_copies(step + 1, lambda c: c.start())

        @pl.when(step == steps - 1)
        def _():
            col_copies(0, lambda c: c.start())

        @pl.when(step < steps)
        def _():
            row_copies(step, lambda c: c.wait())
            slot = lax.rem(step, 2)
            h = hidden_buf[slot].reshape(block, width)
            o = grad_buf[slot].reshape(block, width)
            gate = dot(weights[0][...], h, 1, 1)
            up = dot(weights[1][...], h, 1, 1)
            back = dot(weights[2][...], o, 1, 1)
            sig = jax.nn.sigmoid(gate)
            silu = gate * sig
            kept[0][step] = (silu * up).astype(bf16)
            kept[1][step] = (back * up * sig * (1.0 + gate * (1.0 - sig))).astype(bf16)
            kept[2][step] = (back * silu).astype(bf16)

        @pl.when(step >= steps)
        def _():
            chunk = step - steps
            col_copies(chunk, lambda c: c.wait())

            @pl.when(chunk + 1 < chunks)
            def _():
                col_copies(chunk + 1, lambda c: c.start())

            slot = lax.rem(chunk, 2)
            h = hidden_cols[slot].reshape(steps * block, columns_at_once)
            o = grad_cols[slot].reshape(steps * block, columns_at_once)
            for i, right in ((0, o), (1, h), (2, h)):
                parts = [dot(kept[i][j], right[j * block : (j + 1) * block], 1, 0) for j in range(steps)]
                outs[i][...] = sum(parts[1:], parts[0])

    anywhere = pl.BlockSpec(memory_space=pl.ANY)
    weight = pl.BlockSpec((units, width), lambda i, order: (0, 0), pipeline_mode=pl.Buffered(1))
    result = pl.BlockSpec((units, columns_at_once), lambda i, order: (0, jnp.maximum(i - steps, 0)))
    whole_rows = pltpu.VMEM((2, 2, rows, width), bf16)
    some_columns = pltpu.VMEM((2, 2 * steps, rows, columns_at_once), bf16)
    return pl.pallas_call(
        kernel,
        out_shape=[jax.ShapeDtypeStruct((units, width), f32)] * 3,
        grid_spec=pltpu.PrefetchScalarGridSpec(
            num_scalar_prefetch=1,
            grid=(steps + chunks,),
            in_specs=[anywhere] * (1 + count) + [weight] * 3,
            out_specs=[result] * 3,
            scratch_shapes=[pltpu.VMEM((steps, units, block), bf16)] * 3
            + [whole_rows, whole_rows, some_columns, some_columns]
            + [pltpu.SemaphoreType.DMA((2, 2, 2)), pltpu.SemaphoreType.DMA((2, 2, 2 * steps))],
        ),
        compiler_params=pltpu.CompilerParams(vmem_limit_bytes=60 * 2**20),
        name="feed_forward_grads",
    )(order, hidden_blocks, *grad_pieces, gate_weight, up_weight, down_weight)


def whole_block(shape):
    return pl.BlockSpec(shape, lambda *_: (0,) * len(shape), pipeline_mode=pl.Buffered(1))


def kernel_params(mebibytes=56):
    return pltpu.CompilerParams(vmem_limit_bytes=mebibytes * 2**20)


def row_scale(value):
    return lax.rsqrt(jnp.mean(value * value, axis=-1, keepdims=True) + epsilon)


def normed_projections(inputs, gain_row, weights):
    tok_count, width = inputs.shape
    rows, half = tok_count // 4, weights.shape[2] // 2

    def kernel(inputs_ref, gain_ref, weights_ref, normed_ref, first_ref, second_ref):
        value = inputs_ref[...].astype(f32)
        normed = (value * row_scale(value) * gain_ref[...]).astype(bf16)
        normed_ref[...] = normed
        for which, out in enumerate((first_ref, second_ref)):
            product = dot(normed, weights_ref[which], 1, 0).astype(bf16)
            out[0] = product[:, :half]
            out[1] = product[:, half:]

    halves = jax.ShapeDtypeStruct((2, tok_count, half), bf16)
    halves_block = pl.BlockSpec((2, rows, half), lambda i: (0, i, 0))
    row_block = pl.BlockSpec((rows, width), lambda i: (i, 0))
    return pl.pallas_call(
        kernel,
        out_shape=[jax.ShapeDtypeStruct(inputs.shape, bf16), halves, halves],
        grid=(4,),
        in_specs=[row_block, whole_block((1, width)), whole_block(weights.shape)],
        out_specs=[row_block, halves_block, halves_block],
        compiler_params=kernel_params(),
        name="normed_projections",
    )(inputs, gain_row[None], weights)


def allowed_pairs(seg_column, seg_row, start, rows):
    last = start + rows
    shape = (rows, last)
    places = lax.broadcasted_iota(jnp.int32, shape, 0) + start
    causal = lax.broadcasted_iota(jnp.int32, shape, 1) <= places
    return causal & (seg_column[start:last] == seg_row[:, :last])


def attend_forward(queries, keys, values, out_weight, seg_ids):
    tok_count, flat = queries.shape
    width, heads, rows = out_weight.shape[0], flat // HEAD_SIZE, tok_count // 4

    def kernel(q_ref, k_ref, v_ref, weight_ref, column_ref, row_ref, out_ref, branch_ref, log_ref):
        seg_column, seg_row = column_ref[...], row_ref[...]
        for start in range(0, tok_count, rows):
            last = start + rows
            allowed = allowed_pairs(seg_column, seg_row, start, rows)
            for head in range(heads):
                at = slice(head * HEAD_SIZE, (head + 1) * HEAD_SIZE)
                scores = dot(q_ref[start:last, at], k_ref[:last, at], 1, 1) * HEAD_SIZE ** (-0.5)
                scores = jnp.where(allowed, scores, negative)
                maximum = jnp.max(scores, axis=-1, keepdims=True)
                exponent = jnp.exp(scores - maximum)
                total = jnp.sum(exponent, axis=-1, keepdims=True)
                probs = (exponent * (1.0 / total)).astype(bf16)
                out_ref[start:last, at] = dot(probs, v_ref[:last, at], 1, 0).astype(bf16)
                log_ref[head, start:last] = maximum + jnp.log(total)
            branch_ref[start:last] = dot(out_ref[start:last], weight_ref[...], 1, 1).astype(bf16)

    shapes = [(tok_count, flat), (tok_count, width), (heads, tok_count, 1)]
    return pl.pallas_call(
        kernel,
        out_shape=[jax.ShapeDtypeStruct(s, k) for s, k in zip(shapes, (bf16, bf16, f32))],
        compiler_params=kernel_params(),
        name="attend_forward",
    )(queries, keys, values, out_weight, seg_ids[:, None], seg_ids[None])


def attend_backward(queries, keys, values, out_weight, grad_branch, seg_ids, log_total):
    tok_count, flat = queries.shape
    heads, rows = flat // HEAD_SIZE, tok_count // 4
    scale = HEAD_SIZE ** (-0.5)

    def kernel(q_ref, k_ref, v_ref, weight_ref, branch_ref, column_ref, row_ref, log_ref, dq_ref, dk_ref, dv_ref, dk_sum, dv_sum):
        seg_column, seg_row = column_ref[...], row_ref[...]
        dk_sum[...] = jnp.zeros_like(dk_sum)
        dv_sum[...] = jnp.zeros_like(dv_sum)
        for start in range(0, tok_count, rows):
            last = start + rows
            allowed = allowed_pairs(seg_column, seg_row, start, rows)
            grad_out = dot(branch_ref[start:last], weight_ref[...], 1, 0).astype(bf16)
            for head in range(heads):
                at = slice(head * HEAD_SIZE, (head + 1) * HEAD_SIZE)
                scores = dot(q_ref[start:last, at], k_ref[:last, at], 1, 1) * scale
                probs = jnp.exp(jnp.where(allowed, scores, negative) - log_ref[head, start:last])
                grad_probs = dot(grad_out[:, at], v_ref[:last, at], 1, 1)
                inner = jnp.sum(probs * grad_probs, axis=-1, keepdims=True)
                grad_scores = (probs * (grad_probs - inner)).astype(bf16)
                dq_ref[start:last, at] = (dot(grad_scores, k_ref[:last, at], 1, 0) * scale).astype(bf16)
                dk_sum[:last, at] += dot(grad_scores, q_ref[start:last, at], 0, 0)
                dv_sum[:last, at] += dot(probs.astype(bf16), grad_out[:, at], 0, 0)
        dk_ref[...] = (dk_sum[...] * scale).astype(bf16)
        dv_ref[...] = dv_sum[...].astype(bf16)

    return pl.pallas_call(
        kernel,
        out_shape=[jax.ShapeDtypeStruct((tok_count, flat), bf16)] * 3,
        scratch_shapes=[pltpu.VMEM((tok_count, flat), f32)] * 2,
        compiler_params=kernel_params(),
        name="attend_backward",
    )(queries, keys, values, out_weight, grad_branch, seg_ids[:, None], seg_ids[None], log_total)


def feed_forward_own(hidden_in, grad_hidden, gate_weight, up_weight):
    tok_count, width = hidden_in.shape
    units, rows = gate_weight.shape[0], tok_count // 4

    def kernel(in_ref, back_ref, gate_ref, up_ref, hidden_ref, grad_ref):
        gate = dot(in_ref[...], gate_ref[...], 1, 1)
        up = dot(in_ref[...], up_ref[...], 1, 1)
        back = back_ref[...]
        sig = jax.nn.sigmoid(gate)
        silu = gate * sig
        hidden_ref[...] = (silu * up).astype(bf16)
        grad_up = (back * silu).astype(bf16)
        grad_gate = (back * up * sig * (1.0 + gate * (1.0 - sig))).astype(bf16)
        grad = dot(grad_gate, gate_ref[...], 1, 0) + dot(grad_up, up_ref[...], 1, 0)
        grad_ref[...] = grad.astype(bf16)

    row_block = pl.BlockSpec((rows, width), lambda i: (i, 0))
    unit_block = pl.BlockSpec((rows, units), lambda i: (i, 0))
    weight = whole_block((units, width))
    return pl.pallas_call(
        kernel,
        out_shape=[jax.ShapeDtypeStruct((tok_count, units), bf16), jax.ShapeDtypeStruct((tok_count, width), bf16)],
        grid=(4,),
        in_specs=[row_block, unit_block, weight, weight],
        out_specs=[unit_block, row_block],
        compiler_params=kernel_params(),
        name="feed_forward_own",
    )(hidden_in, grad_hidden, gate_weight, up_weight)


def input_gradient(inputs, gain_row, first_grad, value_grad, weights, parts):
    tok_count, width = inputs.shape
    rows, columns, inner = tok_count // 4, width // parts, first_grad.shape[1]

    def kernel(inputs_ref, gain_ref, first_ref, value_ref, weights_ref, out_ref, gain_out):
        grad = dot(first_ref[...], weights_ref[0], 1, 1) + dot(value_ref[...], weights_ref[1], 1, 1)
        value = inputs_ref[...].astype(f32)
        inverse = row_scale(value)
        normal = value * inverse

        @pl.when(pl.program_id(0) == 0)
        def _():
            gain_out[...] = jnp.zeros_like(gain_out)

        gain_out[...] += jnp.sum(grad * normal, axis=0, keepdims=True)
        scaled = grad * gain_ref[...]
        inner_mean = jnp.mean(scaled * value, axis=-1, keepdims=True)
        result = (inverse * scaled - value * (inverse * inverse * inverse * inner_mean)).astype(bf16)
        for part in range(parts):
            out_ref[part] = result[:, part * columns : (part + 1) * columns]

    row_block = pl.BlockSpec((rows, width), lambda i: (i, 0))
    grad_block = pl.BlockSpec((rows, inner), lambda i: (i, 0))
    return pl.pallas_call(
        kernel,
        out_shape=[jax.ShapeDtypeStruct((parts, tok_count, columns), bf16), jax.ShapeDtypeStruct((1, width), f32)],
        grid=(4,),
        in_specs=[row_block, whole_block((1, width)), grad_block, grad_block, whole_block(weights.shape)],
        out_specs=[pl.BlockSpec((parts, rows, columns), lambda i: (0, i, 0)), pl.BlockSpec((1, width), lambda i: (0, 0))],
        compiler_params=kernel_params(),
        name="input_gradient",
    )(inputs, gain_row[None], first_grad, value_grad, weights)


def output_parts(hidden, down_weight, parts):
    tok_count, units = hidden.shape
    columns = down_weight.shape[1] // parts

    def kernel(hidden_ref, weight_ref, out_ref):
        out_ref[0] = dot(hidden_ref[...], weight_ref[...], 1, 0).astype(bf16)

    return pl.pallas_call(
        kernel,
        out_shape=jax.ShapeDtypeStruct((parts, tok_count, columns), bf16),
        grid=(parts,),
        in_specs=[whole_block((tok_count, units)), pl.BlockSpec((units, columns), lambda i: (0, i))],
        out_specs=pl.BlockSpec((1, tok_count, columns), lambda i: (i, 0, 0)),
        compiler_params=kernel_params(),
        name="output_parts",
    )(hidden, down_weight)


def gathers(group_count):
    return group_count in (2, 4)


def sum_plane(value):
    value = value + swap_section(value)
    both = lax.ppermute(value, "tensor", [(i, i ^ 3) for i in range(4)])
    return value, swap_low(value), swap_high(value), both


def sum_pairs(terms):
    return (terms[0] + terms[1]) + (terms[2] + terms[3])


def sum_over_groups(value):
    count = lax.axis_size("dp")

    def across(distance):
        return lax.ppermute(value, "dp", [(i, i ^ distance) for i in range(count)])

    if count == 4:
        return sum_pairs([value, across(1), across(2), across(3)])
    if count & (count - 1):
        return lax.psum(value, "dp")
    for bit in range(count.bit_length() - 1):
        value = value + across(2**bit)
    return value


def sum_groups(*grads):
    return [g.astype(f32) for g in lax.psum(tuple(g.astype(bf16) for g in grads), "dp")]


def shards(
    block_input,
    out_grad,
    seq_lengths,
    attn_gains,
    attn_weights,
    ffn_gain,
    gate_weight,
    up_weight,
    down_weight,
):
    tok_count, width = block_input.shape
    section = lax.axis_index("section")
    is_first = section == 0
    plane = lax.axis_size("section") * lax.axis_size("tensor")
    plane_pos = section * lax.axis_size("tensor") + lax.axis_index("tensor")
    rows, columns = tok_count // plane, width // plane
    row_start = plane_pos * rows

    def own_rows(value):
        return lax.dynamic_slice_in_dim(value, row_start, rows, 0)

    all_tokens = gathers(lax.axis_size("dp"))
    grad_slices, grad_near = None, []
    if all_tokens:
        grad_slice, block_input = meet(tensor_rows(out_grad), block_input)
        grad_slices = lax.all_gather(grad_slice, "dp", axis=0, tiled=False)
    seg_ids = segment_ids(seq_lengths[0], tok_count)
    is_valid = (seg_ids < seq_lengths.shape[1]).astype(f32)[:, None]
    gain_row = attn_gains[0].astype(f32)
    weights = attn_weights[0]
    w_second = weights[1]
    half = weights.shape[2] // 2
    normed, first_proj, second_proj = normed_projections(block_input, gain_row, weights)

    first_own, first_met = pick(first_proj, section), swap_section(pick(first_proj, 1 - section))
    second_met = lax.ppermute(second_proj[1], "section", [(0, 1)])
    out_weight_met = lax.ppermute(w_second[:, :half], "section", [(1, 0)])
    queries = jnp.where(is_first, first_met, first_own)
    keys = jnp.where(is_first, first_own, first_met)
    values = jnp.where(is_first, second_proj[0], second_met)
    out_weight = jnp.where(is_first, out_weight_met, w_second[:, half:])

    attn_out, branch_part, log_total = attend_forward(queries, keys, values, out_weight, seg_ids)
    branch = scatter_sum(branch_part.reshape(plane, rows, width))
    branch, grad_slices = meet(branch, grad_slices)
    residual = own_rows(block_input).astype(f32) + branch
    resid_inv = lax.rsqrt(jnp.mean(residual * residual, axis=-1, keepdims=True) + epsilon)
    gain_ffn = ffn_gain.astype(f32)
    hidden_block = (residual * resid_inv * gain_ffn).astype(bf16)
    hidden_in = gather_plane(hidden_block)
    if all_tokens:
        hidden_block, grad_slices = meet(hidden_block, grad_slices)
        hidden_all = lax.all_gather(hidden_block, ("dp", "section", "tensor"), axis=0, tiled=True)
        grad_near = other_groups(grad_slices)
        grad_near, hidden_in = meet(grad_near, hidden_in)
    branch_sq = jnp.sum(branch * branch * own_rows(is_valid))

    def whole_units(hidden_in, out_grad):
        gate_act, up_act = dot(hidden_in, gate_weight, 1, 0), dot(hidden_in, up_weight, 1, 0)
        grad_hidden = dot(out_grad, down_weight, 1, 1)
        sig = jax.nn.sigmoid(gate_act)
        hidden = (gate_act * sig * up_act).astype(bf16)
        grad_up = (grad_hidden * gate_act * sig).astype(bf16)
        grad_gate = (grad_hidden * up_act * sig * (1.0 + gate_act * (1.0 - sig))).astype(bf16)
        return dot(hidden, out_grad, 0, 0), dot(hidden_in, grad_gate, 0, 0), dot(hidden_in, grad_up, 0, 0)

    gate_units, up_units = gate_weight.T, up_weight.T
    hidden, grad_hidden_part = feed_forward_own(hidden_in, dot(out_grad, down_weight, 1, 1), gate_units, up_units)
    grad_half = scatter_half(grad_hidden_part.reshape(plane, rows, width))
    grad_half, hidden = meet(grad_half, hidden)
    grad_terms, output_part = meet(scatter_across(grad_half), output_parts(hidden, down_weight, plane))
    grad_hidden_in = scatter_last(*grad_terms)
    ffn_gain_term = jnp.sum(grad_hidden_in * residual * resid_inv, axis=0)
    grad_residual = own_rows(out_grad).astype(f32) + norm_back(residual, resid_inv, gain_ffn, grad_hidden_in)
    grad_branch_low = gather_plane(grad_residual.astype(bf16))
    if all_tokens:
        grad_near, grad_branch_low = meet(grad_near, grad_branch_low)
        grad_far, grad_near[0] = meet(tensor_rows(out_grad, 2)[None], grad_near[0])
        grad_far = lax.ppermute(grad_far, "dp", [(i, i ^ 1) for i in range(lax.axis_size("dp"))])
        grad_high = [grad_far] + [swap_high(v) for v in grad_near[1:2]]

    def add_own(parts, own):
        own = own.reshape(rows, plane, columns).transpose(1, 0, 2)
        mixed = (lax.dynamic_slice_in_dim(parts, row_start, rows, 1).astype(f32) + own).astype(bf16)
        return lax.dynamic_update_slice_in_dim(parts, mixed, row_start, 1)

    output_half = scatter_half(add_own(output_part, residual))
    grad_q, grad_k, grad_v = attend_backward(
        queries, keys, values, out_weight, grad_branch_low, seg_ids, log_total
    )
    second_back = swap_section(jnp.where(is_first, attn_out, grad_v))

    def joined(own, met):
        return jnp.concatenate([jnp.where(is_first, own, met), jnp.where(is_first, met, own)], axis=1)

    second_right = joined(jnp.where(is_first, grad_v, attn_out), second_back)
    second_left = jnp.where(is_first, normed, grad_branch_low)
    second_sum = dot(second_left, second_right, 0, 0).astype(bf16)
    if len(grad_near) > 2:
        second_back, grad_high, grad_near[2] = meet(second_back, grad_high, grad_near[2])
        grad_high.append(swap_high(grad_near[2]))
    first_back = swap_section(jnp.where(is_first, grad_q, grad_k))
    if len(grad_near) > 2:
        first_back, grad_high = meet(first_back, grad_high)
    first_grad = joined(jnp.where(is_first, grad_k, grad_q), first_back)
    value_grad = jnp.where(is_first, second_right, jnp.zeros_like(second_right))
    first_sum = dot(normed, first_grad, 0, 0).astype(bf16)
    output_half, first_sum, second_sum = meet(output_half, first_sum, second_sum)
    output_terms = scatter_across(output_half)
    if all_tokens:
        first_sum, second_sum, hidden_all = meet(first_sum, second_sum, hidden_all)
        grad_pieces = [by_slice(out_grad)] + grad_near + grad_high
        grad_pieces += [swap_low(v) for v in grad_near] + [swap_low(v) for v in grad_high]
        tensor, group, groups = lax.axis_index("tensor"), lax.axis_index("dp"), lax.axis_size("dp")
        order = [group * 4 + i for i in range(4)]
        order += [(group ^ k) * 4 + (tensor ^ i) for i in (0, 2, 1, 3) for k in range(1, groups)]
        down_grad, gate_grad, up_grad = feed_forward_grads(
            jnp.stack(order).astype(jnp.int32),
            hidden_all.reshape(4 * groups, -1, width),
            grad_pieces,
            gate_units,
            up_units,
            down_weight,
        )
        output_terms, first_grad, value_grad, down_grad = meet(output_terms, first_grad, value_grad, down_grad)
        gate_grad, up_grad = gate_grad.T, up_grad.T
    else:
        down_grad, gate_grad, up_grad = sum_groups(*whole_units(hidden_in, out_grad))
    input_part, attn_gain_term = input_gradient(block_input, gain_row, first_grad, value_grad, weights, plane)
    input_terms = scatter_across(scatter_half(add_own(input_part, grad_residual)))
    output_sum = scatter_last(*output_terms)
    block_output = output_sum.astype(bf16)
    output_sq = jnp.sum(output_sum * output_sum * is_valid)

    count_term = jnp.where(plane_pos == 0, jnp.sum(seq_lengths).astype(f32), 0.0)
    section_rows = jnp.where(
        jnp.arange(2, dtype=jnp.int32)[:, None] == section, attn_gain_term, 0.0
    )
    stat_terms = jnp.pad(jnp.stack([output_sq, branch_sq, count_term]), (0, width - 3))
    terms = jnp.concatenate([section_rows, ffn_gain_term[None, :], stat_terms[None, :]], axis=0)
    gains = sum_plane(terms)
    first_sum, second_sum = lax.psum((first_sum, second_sum), "dp")
    if all_tokens:
        first_sum, second_sum, input_terms, gains = meet(first_sum, second_sum, input_terms, gains)
    input_grad = scatter_last(*input_terms).astype(bf16)
    gains = sum_over_groups(sum_pairs(gains))
    attn_weight_grad = jnp.stack([first_sum, second_sum])[None].astype(f32)

    stats = gains[3]
    attn_gain_grad = lax.dynamic_slice_in_dim(gains, section, 1, 0)
    activation_rms = jnp.sqrt(stats[:2] / (stats[2] * width))
    return (
        block_output,
        input_grad,
        attn_gain_grad,
        attn_weight_grad,
        gains[2],
        gate_grad,
        up_grad,
        down_grad,
        activation_rms,
    )


def solution(mesh):
    both = ("section", "tensor")
    in_specs = (
        P("dp", None),
        P("dp", None),
        P("dp", None),
        P("section", None),
        P("section", None, None, "tensor"),
        P(),
        P(None, both),
        P(None, both),
        P(both, None),
    )
    out_specs = (
        P("dp", both),
        P("dp", both),
        P("section", None),
        P("section", None, None, "tensor"),
        P(),
        P(None, both),
        P(None, both),
        P(both, None),
        P(),
    )
    return jax.shard_map(
        shards, mesh=mesh, in_specs=in_specs, out_specs=out_specs, check_vma=False
    )
```

```python
import jax
import jax.numpy as jnp
from jax import lax
from jax.experimental import pallas as pl
from jax.experimental.pallas import tpu as pltpu
from jax.sharding import PartitionSpec as P

HEAD_SIZE = 128
epsilon = 1e-06
negative = -1e30
bf16 = jnp.bfloat16
f32 = jnp.float32

SWAP_SECTION = [(0, 1), (1, 0)]
SWAP_LOW = [(i, i ^ 1) for i in range(4)]
SWAP_HIGH = [(i, i ^ 2) for i in range(4)]
SWAP_BOTH = [(i, i ^ 6) for i in range(8)]


def place():
    section, tensor = lax.axis_index("section"), lax.axis_index("tensor")
    return section, tensor // 2, tensor % 2


def pick(blocks, index):
    return lax.dynamic_index_in_dim(blocks, index, 0, keepdims=False)


def swap_low(value):
    return lax.ppermute(value, "tensor", SWAP_LOW)


def swap_high(value):
    return lax.ppermute(value, "tensor", SWAP_HIGH)


def swap_section(value):
    return lax.ppermute(value, "section", SWAP_SECTION)


def swap_both(value):
    return lax.ppermute(value, ("section", "tensor"), SWAP_BOTH)


def meet(*values):
    return lax.optimization_barrier(values)


def add_low(left, right):
    return (left.astype(f32) + right.astype(f32)).astype(bf16)


def scatter_half(blocks):
    pairs = blocks.reshape((4, 2) + blocks.shape[1:])
    low = place()[2]
    kept = lax.dynamic_index_in_dim(pairs, low, 1, keepdims=False)
    sent = lax.dynamic_index_in_dim(pairs, 1 - low, 1, keepdims=False)
    [half] = meet(add_low(kept, swap_low(sent)))
    return half


def scatter_across(half):
    section, high, _ = place()

    def toward(a, b):
        return pick(half, (section ^ a) * 2 + (high ^ b))

    mid = half.shape[2] // 2
    across = toward(1, 1)
    left_met, right_met = swap_section(across[:, :mid]), swap_high(across[:, mid:])
    return left_met, right_met, toward(1, 0), toward(0, 1), toward(0, 0)


def scatter_last(left_met, right_met, to_section, to_high, own):
    mid = left_met.shape[1]
    to_section = jnp.concatenate([to_section[:, :mid], add_low(to_section[:, mid:], right_met)], axis=1)
    to_high = jnp.concatenate([add_low(to_high[:, :mid], left_met), to_high[:, mid:]], axis=1)
    from_section, from_high = swap_section(to_section), swap_high(to_high)
    return own.astype(f32) + from_section.astype(f32) + from_high.astype(f32)


def scatter_sum(blocks):
    return scatter_last(*scatter_across(scatter_half(blocks)))


def gather_plane(block):
    section, high, low = place()
    rows, width = block.shape
    mid = width // 2
    by_section, by_high = swap_section(block), swap_high(block)
    across_left, across_right = swap_high(by_section[:, :mid]), swap_section(by_high[:, mid:])
    found = [
        (block, 0, 0, 0),
        (by_section, 1, 0, 0),
        (by_high, 0, 1, 0),
        (across_left, 1, 1, 0),
        (across_right, 1, 1, mid),
    ]
    whole = jnp.zeros((8 * rows, width), block.dtype)
    for value, a, b, column in found:
        other = swap_low(value)
        chip = ((section ^ a) * 2 + (high ^ b)) * 2
        whole = lax.dynamic_update_slice(whole, value, ((chip + low) * rows, column))
        whole = lax.dynamic_update_slice(whole, other, ((chip + 1 - low) * rows, column))
    return whole


def tensor_rows(whole, other=0):
    rows = whole.shape[0] // lax.axis_size("tensor")
    return lax.dynamic_slice_in_dim(whole, (lax.axis_index("tensor") ^ other) * rows, rows, 0)


def other_groups(slices):
    group, count = lax.axis_index("dp"), slices.shape[0]
    return [pick(slices, group ^ k)[None] for k in range(1, count)]


def by_slice(whole):
    return whole.reshape(lax.axis_size("tensor"), -1, whole.shape[1])


def segment_ids(length_row, tok_count):
    slots = length_row.shape[0]
    upto = jnp.arange(slots)[None, :] <= jnp.arange(slots)[:, None]
    seq_ends = jnp.sum(jnp.where(upto, length_row[None, :], 0), axis=1)
    places = jnp.arange(tok_count, dtype=jnp.int32)
    return jnp.sum((places[:, None] >= seq_ends[None, :]).astype(jnp.int32), axis=1)


def norm_back(source, inverse, gain_vec, grad_in):
    scaled = grad_in * gain_vec
    inner_mean = jnp.mean(scaled * source, axis=-1, keepdims=True)
    return inverse * scaled - source * inverse**3 * inner_mean


def dot(left, right, left_dim, right_dim):
    return lax.dot_general(
        left, right, (((left_dim,), (right_dim,)), ((), ())), preferred_element_type=f32
    )


def feed_forward_grads(order, hidden_blocks, grad_pieces, gate_weight, up_weight, down_weight):
    columns_at_once = 256
    count = len(grad_pieces)
    flat = [(at, i) for at, piece in enumerate(grad_pieces) for i in range(piece.shape[0])]
    starts = [flat.index((at, 0)) for at in range(count)]
    rows, width = hidden_blocks.shape[1:]
    units, steps, block = gate_weight.shape[0], len(flat) // 2, 2 * rows
    chunks = width // columns_at_once

    def kernel(order_ref, hidden_ref, *refs):
        grads, refs = refs[:count], refs[count:]
        weights, outs, kept, refs = refs[:3], refs[3:6], refs[6:9], refs[9:]
        hidden_buf, grad_buf, hidden_cols, grad_cols, row_sems, col_sems = refs
        step = pl.program_id(0)

        def row_copies(at, do):
            slot = lax.rem(at, 2)
            for static_at in range(steps):

                @pl.when(at == static_at)
                def _():
                    for i in range(2):
                        segment = static_at * 2 + i
                        piece, index = flat[segment]
                        found = hidden_ref.at[order_ref[segment]]
                        do(pltpu.make_async_copy(found, hidden_buf.at[slot, i], row_sems.at[slot, 0, i]))
                        found = grads[piece].at[index]
                        do(pltpu.make_async_copy(found, grad_buf.at[slot, i], row_sems.at[slot, 1, i]))

        def col_copies(at, do):
            slot = lax.rem(at, 2)
            columns = pl.ds(pl.multiple_of(at * columns_at_once, columns_at_once), columns_at_once)
            for segment in range(2 * steps):
                found = hidden_ref.at[order_ref[segment], :, columns]
                do(pltpu.make_async_copy(found, hidden_cols.at[slot, segment], col_sems.at[slot, 0, segment]))
            for piece in range(count):
                found = grads[piece].at[:, :, columns]
                into = grad_cols.at[slot, pl.ds(starts[piece], grad_pieces[piece].shape[0])]
                do(pltpu.make_async_copy(found, into, col_sems.at[slot, 1, piece]))

        @pl.when(step == 0)
        def _():
            row_copies(step, lambda c: c.start())

        @pl.when(step + 1 < steps)
        def _():
            row_copies(step + 1, lambda c: c.start())

        @pl.when(step == steps - 1)
        def _():
            col_copies(0, lambda c: c.start())

        @pl.when(step < steps)
        def _():
            row_copies(step, lambda c: c.wait())
            slot = lax.rem(step, 2)
            h = hidden_buf[slot].reshape(block, width)
            o = grad_buf[slot].reshape(block, width)
            gate = dot(weights[0][...], h, 1, 1)
            up = dot(weights[1][...], h, 1, 1)
            back = dot(weights[2][...], o, 1, 1)
            sig = jax.nn.sigmoid(gate)
            silu = gate * sig
            kept[0][step] = (silu * up).astype(bf16)
            kept[1][step] = (back * up * sig * (1.0 + gate * (1.0 - sig))).astype(bf16)
            kept[2][step] = (back * silu).astype(bf16)

        @pl.when(step >= steps)
        def _():
            chunk = step - steps
            col_copies(chunk, lambda c: c.wait())

            @pl.when(chunk + 1 < chunks)
            def _():
                col_copies(chunk + 1, lambda c: c.start())

            slot = lax.rem(chunk, 2)
            h = hidden_cols[slot].reshape(steps * block, columns_at_once)
            o = grad_cols[slot].reshape(steps * block, columns_at_once)
            for i, right in ((0, o), (1, h), (2, h)):
                parts = [dot(kept[i][j], right[j * block : (j + 1) * block], 1, 0) for j in range(steps)]
                outs[i][...] = sum(parts[1:], parts[0])

    anywhere = pl.BlockSpec(memory_space=pl.ANY)
    weight = pl.BlockSpec((units, width), lambda i, order: (0, 0), pipeline_mode=pl.Buffered(1))
    result = pl.BlockSpec((units, columns_at_once), lambda i, order: (0, jnp.maximum(i - steps, 0)))
    whole_rows = pltpu.VMEM((2, 2, rows, width), bf16)
    some_columns = pltpu.VMEM((2, 2 * steps, rows, columns_at_once), bf16)
    return pl.pallas_call(
        kernel,
        out_shape=[jax.ShapeDtypeStruct((units, width), f32)] * 3,
        grid_spec=pltpu.PrefetchScalarGridSpec(
            num_scalar_prefetch=1,
            grid=(steps + chunks,),
            in_specs=[anywhere] * (1 + count) + [weight] * 3,
            out_specs=[result] * 3,
            scratch_shapes=[pltpu.VMEM((steps, units, block), bf16)] * 3
            + [whole_rows, whole_rows, some_columns, some_columns]
            + [pltpu.SemaphoreType.DMA((2, 2, 2)), pltpu.SemaphoreType.DMA((2, 2, 2 * steps))],
        ),
        compiler_params=pltpu.CompilerParams(vmem_limit_bytes=60 * 2**20),
        name="feed_forward_grads",
    )(order, hidden_blocks, *grad_pieces, gate_weight, up_weight, down_weight)


def whole_block(shape):
    return pl.BlockSpec(shape, lambda *_: (0,) * len(shape), pipeline_mode=pl.Buffered(1))


def kernel_params(mebibytes=56):
    return pltpu.CompilerParams(vmem_limit_bytes=mebibytes * 2**20)


def row_scale(value):
    return lax.rsqrt(jnp.mean(value * value, axis=-1, keepdims=True) + epsilon)


def normed_projections(inputs, gain_row, weights):
    tok_count, width = inputs.shape
    rows, half = tok_count // 4, weights.shape[2] // 2

    def kernel(inputs_ref, gain_ref, weights_ref, normed_ref, first_ref, second_ref):
        value = inputs_ref[...].astype(f32)
        normed = (value * row_scale(value) * gain_ref[...]).astype(bf16)
        normed_ref[...] = normed
        for which, out in enumerate((first_ref, second_ref)):
            product = dot(normed, weights_ref[which], 1, 0).astype(bf16)
            out[0] = product[:, :half]
            out[1] = product[:, half:]

    halves = jax.ShapeDtypeStruct((2, tok_count, half), bf16)
    halves_block = pl.BlockSpec((2, rows, half), lambda i: (0, i, 0))
    row_block = pl.BlockSpec((rows, width), lambda i: (i, 0))
    return pl.pallas_call(
        kernel,
        out_shape=[jax.ShapeDtypeStruct(inputs.shape, bf16), halves, halves],
        grid=(4,),
        in_specs=[row_block, whole_block((1, width)), whole_block(weights.shape)],
        out_specs=[row_block, halves_block, halves_block],
        compiler_params=kernel_params(),
        name="normed_projections",
    )(inputs, gain_row[None], weights)


def allowed_pairs(seg_column, seg_row, start, rows):
    last = start + rows
    shape = (rows, last)
    places = lax.broadcasted_iota(jnp.int32, shape, 0) + start
    causal = lax.broadcasted_iota(jnp.int32, shape, 1) <= places
    return causal & (seg_column[start:last] == seg_row[:, :last])


def attend_forward(queries, keys, values, out_weight, seg_ids):
    tok_count, flat = queries.shape
    width, heads, rows = out_weight.shape[0], flat // HEAD_SIZE, tok_count // 4

    def kernel(q_ref, k_ref, v_ref, weight_ref, column_ref, row_ref, out_ref, branch_ref, log_ref):
        seg_column, seg_row = column_ref[...], row_ref[...]
        for start in range(0, tok_count, rows):
            last = start + rows
            allowed = allowed_pairs(seg_column, seg_row, start, rows)
            for head in range(heads):
                at = slice(head * HEAD_SIZE, (head + 1) * HEAD_SIZE)
                scores = dot(q_ref[start:last, at], k_ref[:last, at], 1, 1) * HEAD_SIZE ** (-0.5)
                scores = jnp.where(allowed, scores, negative)
                maximum = jnp.max(scores, axis=-1, keepdims=True)
                exponent = jnp.exp(scores - maximum)
                total = jnp.sum(exponent, axis=-1, keepdims=True)
                probs = (exponent * (1.0 / total)).astype(bf16)
                out_ref[start:last, at] = dot(probs, v_ref[:last, at], 1, 0).astype(bf16)
                log_ref[head, start:last] = maximum + jnp.log(total)
            branch_ref[start:last] = dot(out_ref[start:last], weight_ref[...], 1, 1).astype(bf16)

    shapes = [(tok_count, flat), (tok_count, width), (heads, tok_count, 1)]
    return pl.pallas_call(
        kernel,
        out_shape=[jax.ShapeDtypeStruct(s, k) for s, k in zip(shapes, (bf16, bf16, f32))],
        compiler_params=kernel_params(),
        name="attend_forward",
    )(queries, keys, values, out_weight, seg_ids[:, None], seg_ids[None])


def attend_backward(queries, keys, values, out_weight, grad_branch, seg_ids, log_total):
    tok_count, flat = queries.shape
    heads, rows = flat // HEAD_SIZE, tok_count // 4
    scale = HEAD_SIZE ** (-0.5)

    def kernel(q_ref, k_ref, v_ref, weight_ref, branch_ref, column_ref, row_ref, log_ref, dq_ref, dk_ref, dv_ref, dk_sum, dv_sum):
        seg_column, seg_row = column_ref[...], row_ref[...]
        dk_sum[...] = jnp.zeros_like(dk_sum)
        dv_sum[...] = jnp.zeros_like(dv_sum)
        for start in range(0, tok_count, rows):
            last = start + rows
            allowed = allowed_pairs(seg_column, seg_row, start, rows)
            grad_out = dot(branch_ref[start:last], weight_ref[...], 1, 0).astype(bf16)
            for head in range(heads):
                at = slice(head * HEAD_SIZE, (head + 1) * HEAD_SIZE)
                scores = dot(q_ref[start:last, at], k_ref[:last, at], 1, 1) * scale
                probs = jnp.exp(jnp.where(allowed, scores, negative) - log_ref[head, start:last])
                grad_probs = dot(grad_out[:, at], v_ref[:last, at], 1, 1)
                inner = jnp.sum(probs * grad_probs, axis=-1, keepdims=True)
                grad_scores = (probs * (grad_probs - inner)).astype(bf16)
                dq_ref[start:last, at] = (dot(grad_scores, k_ref[:last, at], 1, 0) * scale).astype(bf16)
                dk_sum[:last, at] += dot(grad_scores, q_ref[start:last, at], 0, 0)
                dv_sum[:last, at] += dot(probs.astype(bf16), grad_out[:, at], 0, 0)
        dk_ref[...] = (dk_sum[...] * scale).astype(bf16)
        dv_ref[...] = dv_sum[...].astype(bf16)

    return pl.pallas_call(
        kernel,
        out_shape=[jax.ShapeDtypeStruct((tok_count, flat), bf16)] * 3,
        scratch_shapes=[pltpu.VMEM((tok_count, flat), f32)] * 2,
        compiler_params=kernel_params(),
        name="attend_backward",
    )(queries, keys, values, out_weight, grad_branch, seg_ids[:, None], seg_ids[None], log_total)


def feed_forward_own(hidden_in, grad_hidden, gate_weight, up_weight):
    tok_count, width = hidden_in.shape
    units, rows = gate_weight.shape[0], tok_count // 4

    def kernel(in_ref, back_ref, gate_ref, up_ref, hidden_ref, grad_ref):
        gate = dot(in_ref[...], gate_ref[...], 1, 1)
        up = dot(in_ref[...], up_ref[...], 1, 1)
        back = back_ref[...]
        sig = jax.nn.sigmoid(gate)
        silu = gate * sig
        hidden_ref[...] = (silu * up).astype(bf16)
        grad_up = (back * silu).astype(bf16)
        grad_gate = (back * up * sig * (1.0 + gate * (1.0 - sig))).astype(bf16)
        grad = dot(grad_gate, gate_ref[...], 1, 0) + dot(grad_up, up_ref[...], 1, 0)
        grad_ref[...] = grad.astype(bf16)

    row_block = pl.BlockSpec((rows, width), lambda i: (i, 0))
    unit_block = pl.BlockSpec((rows, units), lambda i: (i, 0))
    weight = whole_block((units, width))
    return pl.pallas_call(
        kernel,
        out_shape=[jax.ShapeDtypeStruct((tok_count, units), bf16), jax.ShapeDtypeStruct((tok_count, width), bf16)],
        grid=(4,),
        in_specs=[row_block, unit_block, weight, weight],
        out_specs=[unit_block, row_block],
        compiler_params=kernel_params(),
        name="feed_forward_own",
    )(hidden_in, grad_hidden, gate_weight, up_weight)


def input_gradient(inputs, gain_row, first_grad, value_grad, weights, parts):
    tok_count, width = inputs.shape
    rows, columns, inner = tok_count // 4, width // parts, first_grad.shape[1]

    def kernel(inputs_ref, gain_ref, first_ref, value_ref, weights_ref, out_ref, gain_out):
        grad = dot(first_ref[...], weights_ref[0], 1, 1) + dot(value_ref[...], weights_ref[1], 1, 1)
        value = inputs_ref[...].astype(f32)
        inverse = row_scale(value)
        normal = value * inverse

        @pl.when(pl.program_id(0) == 0)
        def _():
            gain_out[...] = jnp.zeros_like(gain_out)

        gain_out[...] += jnp.sum(grad * normal, axis=0, keepdims=True)
        scaled = grad * gain_ref[...]
        inner_mean = jnp.mean(scaled * value, axis=-1, keepdims=True)
        result = (inverse * scaled - value * (inverse * inverse * inverse * inner_mean)).astype(bf16)
        for part in range(parts):
            out_ref[part] = result[:, part * columns : (part + 1) * columns]

    row_block = pl.BlockSpec((rows, width), lambda i: (i, 0))
    grad_block = pl.BlockSpec((rows, inner), lambda i: (i, 0))
    return pl.pallas_call(
        kernel,
        out_shape=[jax.ShapeDtypeStruct((parts, tok_count, columns), bf16), jax.ShapeDtypeStruct((1, width), f32)],
        grid=(4,),
        in_specs=[row_block, whole_block((1, width)), grad_block, grad_block, whole_block(weights.shape)],
        out_specs=[pl.BlockSpec((parts, rows, columns), lambda i: (0, i, 0)), pl.BlockSpec((1, width), lambda i: (0, 0))],
        compiler_params=kernel_params(),
        name="input_gradient",
    )(inputs, gain_row[None], first_grad, value_grad, weights)


def output_parts(hidden, down_weight, parts):
    tok_count, units = hidden.shape
    columns = down_weight.shape[1] // parts

    def kernel(hidden_ref, weight_ref, out_ref):
        out_ref[0] = dot(hidden_ref[...], weight_ref[...], 1, 0).astype(bf16)

    return pl.pallas_call(
        kernel,
        out_shape=jax.ShapeDtypeStruct((parts, tok_count, columns), bf16),
        grid=(parts,),
        in_specs=[whole_block((tok_count, units)), pl.BlockSpec((units, columns), lambda i: (0, i))],
        out_specs=pl.BlockSpec((1, tok_count, columns), lambda i: (i, 0, 0)),
        compiler_params=kernel_params(),
        name="output_parts",
    )(hidden, down_weight)


def gathers(group_count):
    return group_count in (2, 4)


def sum_plane(value):
    value = value + swap_section(value)
    both = lax.ppermute(value, "tensor", [(i, i ^ 3) for i in range(4)])
    return value, swap_low(value), swap_high(value), both


def sum_pairs(terms):
    return (terms[0] + terms[1]) + (terms[2] + terms[3])


def sum_over_groups(value):
    count = lax.axis_size("dp")

    def across(distance):
        return lax.ppermute(value, "dp", [(i, i ^ distance) for i in range(count)])

    if count == 4:
        return sum_pairs([value, across(1), across(2), across(3)])
    if count & (count - 1):
        return lax.psum(value, "dp")
    for bit in range(count.bit_length() - 1):
        value = value + across(2**bit)
    return value


def sum_groups(*grads):
    return [g.astype(f32) for g in lax.psum(tuple(g.astype(bf16) for g in grads), "dp")]


def shards(
    block_input,
    out_grad,
    seq_lengths,
    attn_gains,
    attn_weights,
    ffn_gain,
    gate_weight,
    up_weight,
    down_weight,
):
    tok_count, width = block_input.shape
    section = lax.axis_index("section")
    is_first = section == 0
    plane = lax.axis_size("section") * lax.axis_size("tensor")
    plane_pos = section * lax.axis_size("tensor") + lax.axis_index("tensor")
    rows, columns = tok_count // plane, width // plane
    row_start = plane_pos * rows

    def own_rows(value):
        return lax.dynamic_slice_in_dim(value, row_start, rows, 0)

    all_tokens = gathers(lax.axis_size("dp"))
    grad_slices, grad_near = None, []
    if all_tokens:
        grad_slice, block_input = meet(tensor_rows(out_grad), block_input)
        grad_slices = lax.all_gather(grad_slice, "dp", axis=0, tiled=False)
    seg_ids = segment_ids(seq_lengths[0], tok_count)
    is_valid = (seg_ids < seq_lengths.shape[1]).astype(f32)[:, None]
    gain_row = attn_gains[0].astype(f32)
    weights = attn_weights[0]
    w_second = weights[1]
    half = weights.shape[2] // 2
    normed, first_proj, second_proj = normed_projections(block_input, gain_row, weights)

    first_own, first_met = pick(first_proj, section), swap_section(pick(first_proj, 1 - section))
    second_met = lax.ppermute(second_proj[1], "section", [(0, 1)])
    out_weight_met = lax.ppermute(w_second[:, :half], "section", [(1, 0)])
    queries = jnp.where(is_first, first_met, first_own)
    keys = jnp.where(is_first, first_own, first_met)
    values = jnp.where(is_first, second_proj[0], second_met)
    out_weight = jnp.where(is_first, out_weight_met, w_second[:, half:])

    attn_out, branch_part, log_total = attend_forward(queries, keys, values, out_weight, seg_ids)
    branch = scatter_sum(branch_part.reshape(plane, rows, width))
    branch, grad_slices = meet(branch, grad_slices)
    residual = own_rows(block_input).astype(f32) + branch
    resid_inv = lax.rsqrt(jnp.mean(residual * residual, axis=-1, keepdims=True) + epsilon)
    gain_ffn = ffn_gain.astype(f32)
    hidden_block = (residual * resid_inv * gain_ffn).astype(bf16)
    hidden_in = gather_plane(hidden_block)
    if all_tokens:
        hidden_block, grad_slices = meet(hidden_block, grad_slices)
        hidden_all = lax.all_gather(hidden_block, ("dp", "section", "tensor"), axis=0, tiled=True)
        grad_near = other_groups(grad_slices)
        grad_near, hidden_in = meet(grad_near, hidden_in)
    branch_sq = jnp.sum(branch * branch * own_rows(is_valid))

    def whole_units(hidden_in, out_grad):
        gate_act, up_act = dot(hidden_in, gate_weight, 1, 0), dot(hidden_in, up_weight, 1, 0)
        grad_hidden = dot(out_grad, down_weight, 1, 1)
        sig = jax.nn.sigmoid(gate_act)
        hidden = (gate_act * sig * up_act).astype(bf16)
        grad_up = (grad_hidden * gate_act * sig).astype(bf16)
        grad_gate = (grad_hidden * up_act * sig * (1.0 + gate_act * (1.0 - sig))).astype(bf16)
        return dot(hidden, out_grad, 0, 0), dot(hidden_in, grad_gate, 0, 0), dot(hidden_in, grad_up, 0, 0)

    gate_units, up_units = gate_weight.T, up_weight.T
    hidden, grad_hidden_part = feed_forward_own(hidden_in, dot(out_grad, down_weight, 1, 1), gate_units, up_units)
    grad_half = scatter_half(grad_hidden_part.reshape(plane, rows, width))
    grad_half, hidden = meet(grad_half, hidden)
    grad_terms, output_part = meet(scatter_across(grad_half), output_parts(hidden, down_weight, plane))
    grad_hidden_in = scatter_last(*grad_terms)
    ffn_gain_term = jnp.sum(grad_hidden_in * residual * resid_inv, axis=0)
    grad_residual = own_rows(out_grad).astype(f32) + norm_back(residual, resid_inv, gain_ffn, grad_hidden_in)
    grad_branch_low = gather_plane(grad_residual.astype(bf16))
    if all_tokens:
        grad_near, grad_branch_low = meet(grad_near, grad_branch_low)
        grad_far, grad_near[0] = meet(tensor_rows(out_grad, 2)[None], grad_near[0])
        grad_far = lax.ppermute(grad_far, "dp", [(i, i ^ 1) for i in range(lax.axis_size("dp"))])
        grad_high = [grad_far] + [swap_high(v) for v in grad_near[1:2]]

    def add_own(parts, own):
        own = own.reshape(rows, plane, columns).transpose(1, 0, 2)
        mixed = (lax.dynamic_slice_in_dim(parts, row_start, rows, 1).astype(f32) + own).astype(bf16)
        return lax.dynamic_update_slice_in_dim(parts, mixed, row_start, 1)

    output_half = scatter_half(add_own(output_part, residual))
    grad_q, grad_k, grad_v = attend_backward(
        queries, keys, values, out_weight, grad_branch_low, seg_ids, log_total
    )
    second_back = swap_section(jnp.where(is_first, attn_out, grad_v))

    def joined(own, met):
        return jnp.concatenate([jnp.where(is_first, own, met), jnp.where(is_first, met, own)], axis=1)

    second_right = joined(jnp.where(is_first, grad_v, attn_out), second_back)
    second_left = jnp.where(is_first, normed, grad_branch_low)
    second_sum = dot(second_left, second_right, 0, 0).astype(bf16)
    if len(grad_near) > 2:
        grad_q, grad_k, grad_high[1], grad_near[2] = meet(grad_q, grad_k, grad_high[1], grad_near[2])
        grad_high.append(swap_high(grad_near[2]))
    first_back = swap_section(jnp.where(is_first, grad_q, grad_k))
    if len(grad_near) > 2:
        first_back, grad_high = meet(first_back, grad_high)
    first_grad = joined(jnp.where(is_first, grad_k, grad_q), first_back)
    value_grad = jnp.where(is_first, second_right, jnp.zeros_like(second_right))
    first_sum = dot(normed, first_grad, 0, 0).astype(bf16)
    output_half, first_sum, second_sum = meet(output_half, first_sum, second_sum)
    output_terms = scatter_across(output_half)
    if all_tokens:
        first_sum, second_sum, hidden_all = meet(first_sum, second_sum, hidden_all)
        grad_pieces = [by_slice(out_grad)] + grad_near + grad_high
        grad_pieces += [swap_low(v) for v in grad_near] + [swap_low(v) for v in grad_high]
        tensor, group, groups = lax.axis_index("tensor"), lax.axis_index("dp"), lax.axis_size("dp")
        order = [group * 4 + i for i in range(4)]
        order += [(group ^ k) * 4 + (tensor ^ i) for i in (0, 2, 1, 3) for k in range(1, groups)]
        down_grad, gate_grad, up_grad = feed_forward_grads(
            jnp.stack(order).astype(jnp.int32),
            hidden_all.reshape(4 * groups, -1, width),
            grad_pieces,
            gate_units,
            up_units,
            down_weight,
        )
        output_terms, first_grad, value_grad, down_grad = meet(output_terms, first_grad, value_grad, down_grad)
        gate_grad, up_grad = gate_grad.T, up_grad.T
    else:
        down_grad, gate_grad, up_grad = sum_groups(*whole_units(hidden_in, out_grad))
    input_part, attn_gain_term = input_gradient(block_input, gain_row, first_grad, value_grad, weights, plane)
    input_terms = scatter_across(scatter_half(add_own(input_part, grad_residual)))
    output_sum = scatter_last(*output_terms)
    block_output = output_sum.astype(bf16)
    output_sq = jnp.sum(output_sum * output_sum * is_valid)

    count_term = jnp.where(plane_pos == 0, jnp.sum(seq_lengths).astype(f32), 0.0)
    section_rows = jnp.where(
        jnp.arange(2, dtype=jnp.int32)[:, None] == section, attn_gain_term, 0.0
    )
    stat_terms = jnp.pad(jnp.stack([output_sq, branch_sq, count_term]), (0, width - 3))
    terms = jnp.concatenate([section_rows, ffn_gain_term[None, :], stat_terms[None, :]], axis=0)
    gains = sum_plane(terms)
    first_sum, second_sum = lax.psum((first_sum, second_sum), "dp")
    if all_tokens:
        first_sum, second_sum, input_terms, gains = meet(first_sum, second_sum, input_terms, gains)
    input_grad = scatter_last(*input_terms).astype(bf16)
    gains = sum_over_groups(sum_pairs(gains))
    attn_weight_grad = jnp.stack([first_sum, second_sum])[None].astype(f32)

    stats = gains[3]
    attn_gain_grad = lax.dynamic_slice_in_dim(gains, section, 1, 0)
    activation_rms = jnp.sqrt(stats[:2] / (stats[2] * width))
    return (
        block_output,
        input_grad,
        attn_gain_grad,
        attn_weight_grad,
        gains[2],
        gate_grad,
        up_grad,
        down_grad,
        activation_rms,
    )


def solution(mesh):
    both = ("section", "tensor")
    in_specs = (
        P("dp", None),
        P("dp", None),
        P("dp", None),
        P("section", None),
        P("section", None, None, "tensor"),
        P(),
        P(None, both),
        P(None, both),
        P(both, None),
    )
    out_specs = (
        P("dp", both),
        P("dp", both),
        P("section", None),
        P("section", None, None, "tensor"),
        P(),
        P(None, both),
        P(None, both),
        P(both, None),
        P(),
    )
    return jax.shard_map(
        shards, mesh=mesh, in_specs=in_specs, out_specs=out_specs, check_vma=False
    )
```

```python
import jax
import jax.numpy as jnp
from jax import lax
from jax.experimental import pallas as pl
from jax.experimental.pallas import tpu as pltpu
from jax.sharding import PartitionSpec as P

HEAD_SIZE = 128
epsilon = 1e-06
negative = -1e30
bf16 = jnp.bfloat16
f32 = jnp.float32

SWAP_SECTION = [(0, 1), (1, 0)]
SWAP_LOW = [(i, i ^ 1) for i in range(4)]
SWAP_HIGH = [(i, i ^ 2) for i in range(4)]
SWAP_BOTH = [(i, i ^ 6) for i in range(8)]


def place():
    section, tensor = lax.axis_index("section"), lax.axis_index("tensor")
    return section, tensor // 2, tensor % 2


def pick(blocks, index):
    return lax.dynamic_index_in_dim(blocks, index, 0, keepdims=False)


def swap_low(value):
    return lax.ppermute(value, "tensor", SWAP_LOW)


def swap_high(value):
    return lax.ppermute(value, "tensor", SWAP_HIGH)


def swap_section(value):
    return lax.ppermute(value, "section", SWAP_SECTION)


def swap_both(value):
    return lax.ppermute(value, ("section", "tensor"), SWAP_BOTH)


def meet(*values):
    return lax.optimization_barrier(values)


def add_low(left, right):
    return (left.astype(f32) + right.astype(f32)).astype(bf16)


def scatter_half(blocks):
    pairs = blocks.reshape((4, 2) + blocks.shape[1:])
    low = place()[2]
    kept = lax.dynamic_index_in_dim(pairs, low, 1, keepdims=False)
    sent = lax.dynamic_index_in_dim(pairs, 1 - low, 1, keepdims=False)
    [half] = meet(add_low(kept, swap_low(sent)))
    return half


def scatter_across(half):
    section, high, _ = place()

    def toward(a, b):
        return pick(half, (section ^ a) * 2 + (high ^ b))

    mid = half.shape[2] // 2
    across = toward(1, 1)
    left_met, right_met = swap_section(across[:, :mid]), swap_high(across[:, mid:])
    return left_met, right_met, toward(1, 0), toward(0, 1), toward(0, 0)


def scatter_last(left_met, right_met, to_section, to_high, own):
    mid = left_met.shape[1]
    to_section = jnp.concatenate([to_section[:, :mid], add_low(to_section[:, mid:], right_met)], axis=1)
    to_high = jnp.concatenate([add_low(to_high[:, :mid], left_met), to_high[:, mid:]], axis=1)
    from_section, from_high = swap_section(to_section), swap_high(to_high)
    return own.astype(f32) + from_section.astype(f32) + from_high.astype(f32)


def scatter_sum(blocks):
    return scatter_last(*scatter_across(scatter_half(blocks)))


def gather_plane(block):
    section, high, low = place()
    rows, width = block.shape
    mid = width // 2
    by_section, by_high = swap_section(block), swap_high(block)
    across_left, across_right = swap_high(by_section[:, :mid]), swap_section(by_high[:, mid:])
    found = [
        (block, 0, 0, 0),
        (by_section, 1, 0, 0),
        (by_high, 0, 1, 0),
        (across_left, 1, 1, 0),
        (across_right, 1, 1, mid),
    ]
    whole = jnp.zeros((8 * rows, width), block.dtype)
    for value, a, b, column in found:
        other = swap_low(value)
        chip = ((section ^ a) * 2 + (high ^ b)) * 2
        whole = lax.dynamic_update_slice(whole, value, ((chip + low) * rows, column))
        whole = lax.dynamic_update_slice(whole, other, ((chip + 1 - low) * rows, column))
    return whole


def tensor_rows(whole, other=0):
    rows = whole.shape[0] // lax.axis_size("tensor")
    return lax.dynamic_slice_in_dim(whole, (lax.axis_index("tensor") ^ other) * rows, rows, 0)


def other_groups(slices):
    group, count = lax.axis_index("dp"), slices.shape[0]
    return [pick(slices, group ^ k)[None] for k in range(1, count)]


def by_slice(whole):
    return whole.reshape(lax.axis_size("tensor"), -1, whole.shape[1])


def segment_ids(length_row, tok_count):
    slots = length_row.shape[0]
    upto = jnp.arange(slots)[None, :] <= jnp.arange(slots)[:, None]
    seq_ends = jnp.sum(jnp.where(upto, length_row[None, :], 0), axis=1)
    places = jnp.arange(tok_count, dtype=jnp.int32)
    return jnp.sum((places[:, None] >= seq_ends[None, :]).astype(jnp.int32), axis=1)


def norm_back(source, inverse, gain_vec, grad_in):
    scaled = grad_in * gain_vec
    inner_mean = jnp.mean(scaled * source, axis=-1, keepdims=True)
    return inverse * scaled - source * inverse**3 * inner_mean


def dot(left, right, left_dim, right_dim):
    return lax.dot_general(
        left, right, (((left_dim,), (right_dim,)), ((), ())), preferred_element_type=f32
    )


def feed_forward_grads(order, hidden_blocks, grad_pieces, gate_weight, up_weight, down_weight):
    columns_at_once = 256
    count = len(grad_pieces)
    flat = [(at, i) for at, piece in enumerate(grad_pieces) for i in range(piece.shape[0])]
    starts = [flat.index((at, 0)) for at in range(count)]
    rows, width = hidden_blocks.shape[1:]
    units, steps, block = gate_weight.shape[0], len(flat) // 2, 2 * rows
    chunks = width // columns_at_once

    def kernel(order_ref, hidden_ref, *refs):
        grads, refs = refs[:count], refs[count:]
        weights, outs, kept, refs = refs[:3], refs[3:6], refs[6:9], refs[9:]
        hidden_buf, grad_buf, hidden_cols, grad_cols, row_sems, col_sems = refs
        step = pl.program_id(0)

        def row_copies(at, do):
            slot = lax.rem(at, 2)
            for static_at in range(steps):

                @pl.when(at == static_at)
                def _():
                    for i in range(2):
                        segment = static_at * 2 + i
                        piece, index = flat[segment]
                        found = hidden_ref.at[order_ref[segment]]
                        do(pltpu.make_async_copy(found, hidden_buf.at[slot, i], row_sems.at[slot, 0, i]))
                        found = grads[piece].at[index]
                        do(pltpu.make_async_copy(found, grad_buf.at[slot, i], row_sems.at[slot, 1, i]))

        def col_copies(at, do):
            slot = lax.rem(at, 2)
            columns = pl.ds(pl.multiple_of(at * columns_at_once, columns_at_once), columns_at_once)
            for segment in range(2 * steps):
                found = hidden_ref.at[order_ref[segment], :, columns]
                do(pltpu.make_async_copy(found, hidden_cols.at[slot, segment], col_sems.at[slot, 0, segment]))
            for piece in range(count):
                found = grads[piece].at[:, :, columns]
                into = grad_cols.at[slot, pl.ds(starts[piece], grad_pieces[piece].shape[0])]
                do(pltpu.make_async_copy(found, into, col_sems.at[slot, 1, piece]))

        @pl.when(step == 0)
        def _():
            row_copies(step, lambda c: c.start())

        @pl.when(step + 1 < steps)
        def _():
            row_copies(step + 1, lambda c: c.start())

        @pl.when(step == steps - 1)
        def _():
            col_copies(0, lambda c: c.start())

        @pl.when(step < steps)
        def _():
            row_copies(step, lambda c: c.wait())
            slot = lax.rem(step, 2)
            h = hidden_buf[slot].reshape(block, width)
            o = grad_buf[slot].reshape(block, width)
            gate = dot(weights[0][...], h, 1, 1)
            up = dot(weights[1][...], h, 1, 1)
            back = dot(weights[2][...], o, 1, 1)
            sig = jax.nn.sigmoid(gate)
            silu = gate * sig
            kept[0][step] = (silu * up).astype(bf16)
            kept[1][step] = (back * up * sig * (1.0 + gate * (1.0 - sig))).astype(bf16)
            kept[2][step] = (back * silu).astype(bf16)

        @pl.when(step >= steps)
        def _():
            chunk = step - steps
            col_copies(chunk, lambda c: c.wait())

            @pl.when(chunk + 1 < chunks)
            def _():
                col_copies(chunk + 1, lambda c: c.start())

            slot = lax.rem(chunk, 2)
            h = hidden_cols[slot].reshape(steps * block, columns_at_once)
            o = grad_cols[slot].reshape(steps * block, columns_at_once)
            for i, right in ((0, o), (1, h), (2, h)):
                parts = [dot(kept[i][j], right[j * block : (j + 1) * block], 1, 0) for j in range(steps)]
                outs[i][...] = sum(parts[1:], parts[0])

    anywhere = pl.BlockSpec(memory_space=pl.ANY)
    weight = pl.BlockSpec((units, width), lambda i, order: (0, 0), pipeline_mode=pl.Buffered(1))
    result = pl.BlockSpec((units, columns_at_once), lambda i, order: (0, jnp.maximum(i - steps, 0)))
    whole_rows = pltpu.VMEM((2, 2, rows, width), bf16)
    some_columns = pltpu.VMEM((2, 2 * steps, rows, columns_at_once), bf16)
    return pl.pallas_call(
        kernel,
        out_shape=[jax.ShapeDtypeStruct((units, width), f32)] * 3,
        grid_spec=pltpu.PrefetchScalarGridSpec(
            num_scalar_prefetch=1,
            grid=(steps + chunks,),
            in_specs=[anywhere] * (1 + count) + [weight] * 3,
            out_specs=[result] * 3,
            scratch_shapes=[pltpu.VMEM((steps, units, block), bf16)] * 3
            + [whole_rows, whole_rows, some_columns, some_columns]
            + [pltpu.SemaphoreType.DMA((2, 2, 2)), pltpu.SemaphoreType.DMA((2, 2, 2 * steps))],
        ),
        compiler_params=pltpu.CompilerParams(vmem_limit_bytes=60 * 2**20),
        name="feed_forward_grads",
    )(order, hidden_blocks, *grad_pieces, gate_weight, up_weight, down_weight)


def whole_block(shape):
    return pl.BlockSpec(shape, lambda *_: (0,) * len(shape), pipeline_mode=pl.Buffered(1))


def kernel_params(mebibytes=56):
    return pltpu.CompilerParams(vmem_limit_bytes=mebibytes * 2**20)


def row_scale(value):
    return lax.rsqrt(jnp.mean(value * value, axis=-1, keepdims=True) + epsilon)


def normed_projections(inputs, gain_row, weights):
    tok_count, width = inputs.shape
    rows, half = tok_count // 4, weights.shape[2] // 2

    def kernel(inputs_ref, gain_ref, weights_ref, normed_ref, first_ref, second_ref):
        value = inputs_ref[...].astype(f32)
        normed = (value * row_scale(value) * gain_ref[...]).astype(bf16)
        normed_ref[...] = normed
        for which, out in enumerate((first_ref, second_ref)):
            product = dot(normed, weights_ref[which], 1, 0).astype(bf16)
            out[0] = product[:, :half]
            out[1] = product[:, half:]

    halves = jax.ShapeDtypeStruct((2, tok_count, half), bf16)
    halves_block = pl.BlockSpec((2, rows, half), lambda i: (0, i, 0))
    row_block = pl.BlockSpec((rows, width), lambda i: (i, 0))
    return pl.pallas_call(
        kernel,
        out_shape=[jax.ShapeDtypeStruct(inputs.shape, bf16), halves, halves],
        grid=(4,),
        in_specs=[row_block, whole_block((1, width)), whole_block(weights.shape)],
        out_specs=[row_block, halves_block, halves_block],
        compiler_params=kernel_params(),
        name="normed_projections",
    )(inputs, gain_row[None], weights)


def allowed_pairs(seg_column, seg_row, start, rows):
    last = start + rows
    shape = (rows, last)
    places = lax.broadcasted_iota(jnp.int32, shape, 0) + start
    causal = lax.broadcasted_iota(jnp.int32, shape, 1) <= places
    return causal & (seg_column[start:last] == seg_row[:, :last])


def attend_forward(queries, keys, values, out_weight, seg_ids):
    tok_count, flat = queries.shape
    width, heads, rows = out_weight.shape[0], flat // HEAD_SIZE, tok_count // 4

    def kernel(q_ref, k_ref, v_ref, weight_ref, column_ref, row_ref, out_ref, branch_ref, log_ref):
        seg_column, seg_row = column_ref[...], row_ref[...]
        for start in range(0, tok_count, rows):
            last = start + rows
            allowed = allowed_pairs(seg_column, seg_row, start, rows)
            for head in range(heads):
                at = slice(head * HEAD_SIZE, (head + 1) * HEAD_SIZE)
                scores = dot(q_ref[start:last, at], k_ref[:last, at], 1, 1) * HEAD_SIZE ** (-0.5)
                scores = jnp.where(allowed, scores, negative)
                maximum = jnp.max(scores, axis=-1, keepdims=True)
                exponent = jnp.exp(scores - maximum)
                total = jnp.sum(exponent, axis=-1, keepdims=True)
                probs = (exponent * (1.0 / total)).astype(bf16)
                out_ref[start:last, at] = dot(probs, v_ref[:last, at], 1, 0).astype(bf16)
                log_ref[head, start:last] = maximum + jnp.log(total)
            branch_ref[start:last] = dot(out_ref[start:last], weight_ref[...], 1, 1).astype(bf16)

    shapes = [(tok_count, flat), (tok_count, width), (heads, tok_count, 1)]
    return pl.pallas_call(
        kernel,
        out_shape=[jax.ShapeDtypeStruct(s, k) for s, k in zip(shapes, (bf16, bf16, f32))],
        compiler_params=kernel_params(),
        name="attend_forward",
    )(queries, keys, values, out_weight, seg_ids[:, None], seg_ids[None])


def attend_backward(queries, keys, values, out_weight, grad_branch, seg_ids, log_total):
    tok_count, flat = queries.shape
    heads, rows = flat // HEAD_SIZE, tok_count // 4
    scale = HEAD_SIZE ** (-0.5)

    def kernel(q_ref, k_ref, v_ref, weight_ref, branch_ref, column_ref, row_ref, log_ref, dq_ref, dk_ref, dv_ref, dk_sum, dv_sum):
        seg_column, seg_row = column_ref[...], row_ref[...]
        dk_sum[...] = jnp.zeros_like(dk_sum)
        dv_sum[...] = jnp.zeros_like(dv_sum)
        for start in range(0, tok_count, rows):
            last = start + rows
            allowed = allowed_pairs(seg_column, seg_row, start, rows)
            grad_out = dot(branch_ref[start:last], weight_ref[...], 1, 0).astype(bf16)
            for head in range(heads):
                at = slice(head * HEAD_SIZE, (head + 1) * HEAD_SIZE)
                scores = dot(q_ref[start:last, at], k_ref[:last, at], 1, 1) * scale
                probs = jnp.exp(jnp.where(allowed, scores, negative) - log_ref[head, start:last])
                grad_probs = dot(grad_out[:, at], v_ref[:last, at], 1, 1)
                inner = jnp.sum(probs * grad_probs, axis=-1, keepdims=True)
                grad_scores = (probs * (grad_probs - inner)).astype(bf16)
                dq_ref[start:last, at] = (dot(grad_scores, k_ref[:last, at], 1, 0) * scale).astype(bf16)
                dk_sum[:last, at] += dot(grad_scores, q_ref[start:last, at], 0, 0)
                dv_sum[:last, at] += dot(probs.astype(bf16), grad_out[:, at], 0, 0)
        dk_ref[...] = (dk_sum[...] * scale).astype(bf16)
        dv_ref[...] = dv_sum[...].astype(bf16)

    return pl.pallas_call(
        kernel,
        out_shape=[jax.ShapeDtypeStruct((tok_count, flat), bf16)] * 3,
        scratch_shapes=[pltpu.VMEM((tok_count, flat), f32)] * 2,
        compiler_params=kernel_params(),
        name="attend_backward",
    )(queries, keys, values, out_weight, grad_branch, seg_ids[:, None], seg_ids[None], log_total)


def feed_forward_own(hidden_in, grad_hidden, gate_weight, up_weight):
    tok_count, width = hidden_in.shape
    units, rows = gate_weight.shape[0], tok_count // 4

    def kernel(in_ref, back_ref, gate_ref, up_ref, hidden_ref, grad_ref):
        gate = dot(in_ref[...], gate_ref[...], 1, 1)
        up = dot(in_ref[...], up_ref[...], 1, 1)
        back = back_ref[...]
        sig = jax.nn.sigmoid(gate)
        silu = gate * sig
        hidden_ref[...] = (silu * up).astype(bf16)
        grad_up = (back * silu).astype(bf16)
        grad_gate = (back * up * sig * (1.0 + gate * (1.0 - sig))).astype(bf16)
        grad = dot(grad_gate, gate_ref[...], 1, 0) + dot(grad_up, up_ref[...], 1, 0)
        grad_ref[...] = grad.astype(bf16)

    row_block = pl.BlockSpec((rows, width), lambda i: (i, 0))
    unit_block = pl.BlockSpec((rows, units), lambda i: (i, 0))
    weight = whole_block((units, width))
    return pl.pallas_call(
        kernel,
        out_shape=[jax.ShapeDtypeStruct((tok_count, units), bf16), jax.ShapeDtypeStruct((tok_count, width), bf16)],
        grid=(4,),
        in_specs=[row_block, unit_block, weight, weight],
        out_specs=[unit_block, row_block],
        compiler_params=kernel_params(),
        name="feed_forward_own",
    )(hidden_in, grad_hidden, gate_weight, up_weight)


def input_gradient(inputs, gain_row, first_grad, value_grad, weights, parts):
    tok_count, width = inputs.shape
    rows, columns, inner = tok_count // 4, width // parts, first_grad.shape[1]

    def kernel(inputs_ref, gain_ref, first_ref, value_ref, weights_ref, out_ref, gain_out):
        grad = dot(first_ref[...], weights_ref[0], 1, 1) + dot(value_ref[...], weights_ref[1], 1, 1)
        value = inputs_ref[...].astype(f32)
        inverse = row_scale(value)
        normal = value * inverse

        @pl.when(pl.program_id(0) == 0)
        def _():
            gain_out[...] = jnp.zeros_like(gain_out)

        gain_out[...] += jnp.sum(grad * normal, axis=0, keepdims=True)
        scaled = grad * gain_ref[...]
        inner_mean = jnp.mean(scaled * value, axis=-1, keepdims=True)
        result = (inverse * scaled - value * (inverse * inverse * inverse * inner_mean)).astype(bf16)
        for part in range(parts):
            out_ref[part] = result[:, part * columns : (part + 1) * columns]

    row_block = pl.BlockSpec((rows, width), lambda i: (i, 0))
    grad_block = pl.BlockSpec((rows, inner), lambda i: (i, 0))
    return pl.pallas_call(
        kernel,
        out_shape=[jax.ShapeDtypeStruct((parts, tok_count, columns), bf16), jax.ShapeDtypeStruct((1, width), f32)],
        grid=(4,),
        in_specs=[row_block, whole_block((1, width)), grad_block, grad_block, whole_block(weights.shape)],
        out_specs=[pl.BlockSpec((parts, rows, columns), lambda i: (0, i, 0)), pl.BlockSpec((1, width), lambda i: (0, 0))],
        compiler_params=kernel_params(),
        name="input_gradient",
    )(inputs, gain_row[None], first_grad, value_grad, weights)


def output_parts(hidden, down_weight, parts):
    tok_count, units = hidden.shape
    columns = down_weight.shape[1] // parts

    def kernel(hidden_ref, weight_ref, out_ref):
        out_ref[0] = dot(hidden_ref[...], weight_ref[...], 1, 0).astype(bf16)

    return pl.pallas_call(
        kernel,
        out_shape=jax.ShapeDtypeStruct((parts, tok_count, columns), bf16),
        grid=(parts,),
        in_specs=[whole_block((tok_count, units)), pl.BlockSpec((units, columns), lambda i: (0, i))],
        out_specs=pl.BlockSpec((1, tok_count, columns), lambda i: (i, 0, 0)),
        compiler_params=kernel_params(),
        name="output_parts",
    )(hidden, down_weight)


def gathers(group_count):
    return group_count in (2, 4)


def sum_plane(value):
    value = value + swap_section(value)
    both = lax.ppermute(value, "tensor", [(i, i ^ 3) for i in range(4)])
    return value, swap_low(value), swap_high(value), both


def sum_pairs(terms):
    return (terms[0] + terms[1]) + (terms[2] + terms[3])


def sum_over_groups(value):
    count = lax.axis_size("dp")

    def across(distance):
        return lax.ppermute(value, "dp", [(i, i ^ distance) for i in range(count)])

    if count == 4:
        return sum_pairs([value, across(1), across(2), across(3)])
    if count & (count - 1):
        return lax.psum(value, "dp")
    for bit in range(count.bit_length() - 1):
        value = value + across(2**bit)
    return value


def sum_groups(*grads):
    return [g.astype(f32) for g in lax.psum(tuple(g.astype(bf16) for g in grads), "dp")]


def shards(
    block_input,
    out_grad,
    seq_lengths,
    attn_gains,
    attn_weights,
    ffn_gain,
    gate_weight,
    up_weight,
    down_weight,
):
    tok_count, width = block_input.shape
    section = lax.axis_index("section")
    is_first = section == 0
    plane = lax.axis_size("section") * lax.axis_size("tensor")
    plane_pos = section * lax.axis_size("tensor") + lax.axis_index("tensor")
    rows, columns = tok_count // plane, width // plane
    row_start = plane_pos * rows

    def own_rows(value):
        return lax.dynamic_slice_in_dim(value, row_start, rows, 0)

    all_tokens = gathers(lax.axis_size("dp"))
    grad_slices, grad_near = None, []
    if all_tokens:
        grad_slice, block_input = meet(tensor_rows(out_grad), block_input)
        grad_slices = lax.all_gather(grad_slice, "dp", axis=0, tiled=False)
    seg_ids = segment_ids(seq_lengths[0], tok_count)
    is_valid = (seg_ids < seq_lengths.shape[1]).astype(f32)[:, None]
    gain_row = attn_gains[0].astype(f32)
    weights = attn_weights[0]
    w_second = weights[1]
    half = weights.shape[2] // 2
    normed, first_proj, second_proj = normed_projections(block_input, gain_row, weights)

    first_own, first_met = pick(first_proj, section), swap_section(pick(first_proj, 1 - section))
    second_met = lax.ppermute(second_proj[1], "section", [(0, 1)])
    out_weight_met = lax.ppermute(w_second[:, :half], "section", [(1, 0)])
    queries = jnp.where(is_first, first_met, first_own)
    keys = jnp.where(is_first, first_own, first_met)
    values = jnp.where(is_first, second_proj[0], second_met)
    out_weight = jnp.where(is_first, out_weight_met, w_second[:, half:])

    attn_out, branch_part, log_total = attend_forward(queries, keys, values, out_weight, seg_ids)
    branch = scatter_sum(branch_part.reshape(plane, rows, width))
    residual = own_rows(block_input).astype(f32) + branch
    resid_inv = lax.rsqrt(jnp.mean(residual * residual, axis=-1, keepdims=True) + epsilon)
    gain_ffn = ffn_gain.astype(f32)
    hidden_block = (residual * resid_inv * gain_ffn).astype(bf16)
    hidden_block, grad_slices = meet(hidden_block, grad_slices)
    hidden_in = gather_plane(hidden_block)
    if all_tokens:
        hidden_all = lax.all_gather(hidden_block, ("dp", "section", "tensor"), axis=0, tiled=True)
        grad_near = other_groups(grad_slices)
        grad_near, hidden_in = meet(grad_near, hidden_in)
    branch_sq = jnp.sum(branch * branch * own_rows(is_valid))

    def whole_units(hidden_in, out_grad):
        gate_act, up_act = dot(hidden_in, gate_weight, 1, 0), dot(hidden_in, up_weight, 1, 0)
        grad_hidden = dot(out_grad, down_weight, 1, 1)
        sig = jax.nn.sigmoid(gate_act)
        hidden = (gate_act * sig * up_act).astype(bf16)
        grad_up = (grad_hidden * gate_act * sig).astype(bf16)
        grad_gate = (grad_hidden * up_act * sig * (1.0 + gate_act * (1.0 - sig))).astype(bf16)
        return dot(hidden, out_grad, 0, 0), dot(hidden_in, grad_gate, 0, 0), dot(hidden_in, grad_up, 0, 0)

    gate_units, up_units = gate_weight.T, up_weight.T
    hidden, grad_hidden_part = feed_forward_own(hidden_in, dot(out_grad, down_weight, 1, 1), gate_units, up_units)
    grad_half = scatter_half(grad_hidden_part.reshape(plane, rows, width))
    grad_half, hidden = meet(grad_half, hidden)
    grad_terms, output_part = meet(scatter_across(grad_half), output_parts(hidden, down_weight, plane))
    grad_hidden_in = scatter_last(*grad_terms)
    ffn_gain_term = jnp.sum(grad_hidden_in * residual * resid_inv, axis=0)
    grad_residual = own_rows(out_grad).astype(f32) + norm_back(residual, resid_inv, gain_ffn, grad_hidden_in)
    grad_branch_low = gather_plane(grad_residual.astype(bf16))
    if all_tokens:
        grad_near, grad_branch_low = meet(grad_near, grad_branch_low)
        grad_far, grad_near[0] = meet(tensor_rows(out_grad, 2)[None], grad_near[0])
        grad_far = lax.ppermute(grad_far, "dp", [(i, i ^ 1) for i in range(lax.axis_size("dp"))])
        grad_high = [grad_far] + [swap_high(v) for v in grad_near[1:2]]

    def add_own(parts, own):
        own = own.reshape(rows, plane, columns).transpose(1, 0, 2)
        mixed = (lax.dynamic_slice_in_dim(parts, row_start, rows, 1).astype(f32) + own).astype(bf16)
        return lax.dynamic_update_slice_in_dim(parts, mixed, row_start, 1)

    output_half = scatter_half(add_own(output_part, residual))
    grad_q, grad_k, grad_v = attend_backward(
        queries, keys, values, out_weight, grad_branch_low, seg_ids, log_total
    )
    second_back = swap_section(jnp.where(is_first, attn_out, grad_v))

    def joined(own, met):
        return jnp.concatenate([jnp.where(is_first, own, met), jnp.where(is_first, met, own)], axis=1)

    second_right = joined(jnp.where(is_first, grad_v, attn_out), second_back)
    second_left = jnp.where(is_first, normed, grad_branch_low)
    second_sum = dot(second_left, second_right, 0, 0).astype(bf16)
    if len(grad_near) > 2:
        grad_q, grad_k, grad_high[1], grad_near[2] = meet(grad_q, grad_k, grad_high[1], grad_near[2])
        grad_high.append(swap_high(grad_near[2]))
    first_back = swap_section(jnp.where(is_first, grad_q, grad_k))
    if len(grad_near) > 2:
        first_back, grad_high = meet(first_back, grad_high)
    first_grad = joined(jnp.where(is_first, grad_k, grad_q), first_back)
    value_grad = jnp.where(is_first, second_right, jnp.zeros_like(second_right))
    first_sum = dot(normed, first_grad, 0, 0).astype(bf16)
    output_half, first_sum, second_sum = meet(output_half, first_sum, second_sum)
    output_terms = scatter_across(output_half)
    if all_tokens:
        first_sum, second_sum, hidden_all = meet(first_sum, second_sum, hidden_all)
        grad_pieces = [by_slice(out_grad)] + grad_near + grad_high
        grad_pieces += [swap_low(v) for v in grad_near] + [swap_low(v) for v in grad_high]
        tensor, group, groups = lax.axis_index("tensor"), lax.axis_index("dp"), lax.axis_size("dp")
        order = [group * 4 + i for i in range(4)]
        order += [(group ^ k) * 4 + (tensor ^ i) for i in (0, 2, 1, 3) for k in range(1, groups)]
        down_grad, gate_grad, up_grad = feed_forward_grads(
            jnp.stack(order).astype(jnp.int32),
            hidden_all.reshape(4 * groups, -1, width),
            grad_pieces,
            gate_units,
            up_units,
            down_weight,
        )
        output_terms, first_grad, value_grad, down_grad = meet(output_terms, first_grad, value_grad, down_grad)
        gate_grad, up_grad = gate_grad.T, up_grad.T
    else:
        down_grad, gate_grad, up_grad = sum_groups(*whole_units(hidden_in, out_grad))
    input_part, attn_gain_term = input_gradient(block_input, gain_row, first_grad, value_grad, weights, plane)
    input_terms = scatter_across(scatter_half(add_own(input_part, grad_residual)))
    output_sum = scatter_last(*output_terms)
    block_output = output_sum.astype(bf16)
    output_sq = jnp.sum(output_sum * output_sum * is_valid)

    count_term = jnp.where(plane_pos == 0, jnp.sum(seq_lengths).astype(f32), 0.0)
    section_rows = jnp.where(
        jnp.arange(2, dtype=jnp.int32)[:, None] == section, attn_gain_term, 0.0
    )
    stat_terms = jnp.pad(jnp.stack([output_sq, branch_sq, count_term]), (0, width - 3))
    terms = jnp.concatenate([section_rows, ffn_gain_term[None, :], stat_terms[None, :]], axis=0)
    gains = sum_plane(terms)
    first_sum, second_sum = lax.psum((first_sum, second_sum), "dp")
    if all_tokens:
        first_sum, second_sum, input_terms, gains = meet(first_sum, second_sum, input_terms, gains)
    input_grad = scatter_last(*input_terms).astype(bf16)
    gains = sum_over_groups(sum_pairs(gains))
    attn_weight_grad = jnp.stack([first_sum, second_sum])[None].astype(f32)

    stats = gains[3]
    attn_gain_grad = lax.dynamic_slice_in_dim(gains, section, 1, 0)
    activation_rms = jnp.sqrt(stats[:2] / (stats[2] * width))
    return (
        block_output,
        input_grad,
        attn_gain_grad,
        attn_weight_grad,
        gains[2],
        gate_grad,
        up_grad,
        down_grad,
        activation_rms,
    )


def solution(mesh):
    both = ("section", "tensor")
    in_specs = (
        P("dp", None),
        P("dp", None),
        P("dp", None),
        P("section", None),
        P("section", None, None, "tensor"),
        P(),
        P(None, both),
        P(None, both),
        P(both, None),
    )
    out_specs = (
        P("dp", both),
        P("dp", both),
        P("section", None),
        P("section", None, None, "tensor"),
        P(),
        P(None, both),
        P(None, both),
        P(both, None),
        P(),
    )
    return jax.shard_map(
        shards, mesh=mesh, in_specs=in_specs, out_specs=out_specs, check_vma=False
    )
```
